32 devices in a mesh: dp: 8 (over z, y), chan: 4 (over x, core).
Axes of the slice: x: 2, y: 2, z: 4, core: 2. Of those that a mesh axis runs over, the one named last changes fastest.
Arguments:
- features: bfloat16 [128, 10, 10, 2048], P('dp', None, None, 'chan'), may hold values from -6 to 6
- labels: int32 [128], P('dp'), may hold values from 0 to 999
- class_weights: int32 [1000], replicated, may hold values from 1 to 10
- conv_in: float32 [2048, 512], P('dp', 'chan'), may hold values from -0.125 to 0.125
- conv_mid: float32 [3, 3, 512, 512], P(None, None, 'dp', 'chan'), may hold values from -0.09375 to 0.09375
- conv_out: float32 [512, 2048], P('chan', 'dp'), may hold values from -0.25 to 0.25
- classifier: float32 [2048, 1000], P('dp', 'chan'), may hold values from -0.44194174 to 0.44194174
- norms: float32 [2, 4, 768], P(None, 'chan'), may hold values from -1 to 2, as said below
- momentum_in: float32 [2048, 512], P('dp', 'chan'), may hold values from -0.03125 to 0.03125
- momentum_mid: float32 [3, 3, 512, 512], P(None, None, 'dp', 'chan'), may hold values from -0.03125 to 0.03125
- momentum_out: float32 [512, 2048], P('chan', 'dp'), may hold values from -0.03125 to 0.03125
- momentum_head: float32 [2048, 1000], P('dp', 'chan'), may hold values from -0.03125 to 0.03125
- momentum_norms: float32 [2, 4, 768], P(None, 'chan'), may hold values from -0.046875 to 0.046875
- average_in: float32 [2048, 512], P('dp', 'chan'), may hold values from -0.125 to 0.125
- average_mid: float32 [3, 3, 512, 512], P(None, None, 'dp', 'chan'), may hold values from -0.09375 to 0.09375
- average_out: float32 [512, 2048], P('chan', 'dp'), may hold values from -0.25 to 0.25
- average_head: float32 [2048, 1000], P('dp', 'chan'), may hold values from -0.125 to 0.125
- average_norms: float32 [2, 4, 768], P(None, 'chan'), may hold values from 0.5 to 1.5
Outputs:
- loss_sum: float32 [], replicated
- weight_sum: float32 [], replicated
- new_in: float32 [2048, 512], P('dp', 'chan')
- new_mid: float32 [3, 3, 512, 512], P(None, None, 'dp', 'chan')
- new_out: float32 [512, 2048], P('chan', 'dp')
- new_head: float32 [2048, 1000], P('dp', 'chan')
- new_norms: float32 [2, 4, 768], P(None, 'chan')
- fresh_in: float32 [2048, 512], P('dp', 'chan')
- fresh_mid: float32 [3, 3, 512, 512], P(None, None, 'dp', 'chan')
- fresh_out: float32 [512, 2048], P('chan', 'dp')
- fresh_head: float32 [2048, 1000], P('dp', 'chan')
- fresh_norms: float32 [2, 4, 768], P(None, 'chan')
- mean_in: float32 [2048, 512], P('dp', 'chan')
- mean_mid: float32 [3, 3, 512, 512], P(None, None, 'dp', 'chan')
- mean_out: float32 [512, 2048], P('chan', 'dp')
- mean_head: float32 [2048, 1000], P('dp', 'chan')
- mean_norms: float32 [2, 4, 768], P(None, 'chan')
- copy_in: bfloat16 [2048, 512], P('dp', 'chan')
- copy_mid: bfloat16 [3, 3, 512, 512], P(None, None, 'dp', 'chan')
- copy_out: bfloat16 [512, 2048], P('chan', 'dp')
- copy_head: bfloat16 [2048, 1000], P('dp', 'chan')
- copy_norms: bfloat16 [2, 4, 768], P(None, 'chan')
The draws below stay inside these ranges and needn't reach their ends.
Inputs may be any that keep to these rules, and one draw needn't show every extreme that they name: `norms`: gains in row 0, shifts in row 1.
All inputs are finite; a program needn't handle non-finite values.
Results may differ from the reference program's by a relative error of at most 0.025.
Values may be sent and summed in bfloat16 or wider, within the bound.
No kernel may reach another device: no remote copies, remote signals or barrier semaphores. Data moves between devices by JAX's collectives and lax.ppermute only.
A program may use at most 128 MiB of HBM per device.

```python
import jax
import jax.numpy as jnp
from jax import lax

C_IN = 2048
MID = 512
CLASSES = 1000
MAP = 10
IMAGES = 128
N_CHAN = 4


def draw_norms(key, part):
    key = jax.random.fold_in(key, 7)
    first, second = jax.random.split(key)
    width = 2 * MID // N_CHAN + C_IN // N_CHAN
    gain = jax.random.uniform(first, (1, N_CHAN, width), jnp.float32, 0.6, 1.6)
    shift = 0.3 * jax.random.truncated_normal(second, -3.0, 3.0, (1, N_CHAN, width), jnp.float32)
    return jnp.concatenate([gain, shift], axis=0)


def column_scale(rise):
    place = jnp.arange(CLASSES, dtype=jnp.float32) / (CLASSES - 1)
    return 1.6 * (1.0 + rise * place) * C_IN ** (-0.5)


def draw_classifier(key, part):
    key = jax.random.fold_in(key, 11)
    base = jax.random.truncated_normal(key, -4.0, 4.0, (C_IN, CLASSES), jnp.float32)
    return base * column_scale(2.0)[None, :]


def with_ends(result, rng, least, top_value):
    spot = [jax.random.randint(jax.random.fold_in(rng, axis), (), 0, length) for axis, length in enumerate(result.shape)]
    main_axis = result.shape.index(max(result.shape))
    next_to = spot[:main_axis] + [(spot[main_axis] + 1) % result.shape[main_axis]] + spot[main_axis + 1:]
    return result.at[tuple(spot)].set(least).at[tuple(next_to)].set(top_value)


def steps_of(own_key, dims, pieces, smallest, high):
    loudness, own = 1.0, jax.random.fold_in(own_key, 6)
    for position, parts in pieces:
        heights = jnp.exp(jax.random.uniform(jax.random.fold_in(own, position), (parts,), jnp.float32, smallest / len(pieces), high / len(pieces)))
        loudness = loudness * jnp.repeat(heights, dims[position] // parts).reshape([-1 if axis == position else 1 for axis in range(len(dims))])
    return loudness


def noise(key, shape, deviation, most, cuts=(), kind=jnp.bfloat16):
    result = jax.random.normal(key, shape, jnp.float32) * deviation
    if len(cuts) > 0:
        result = steps_of(key, shape, cuts, -0.22, 0.18) * result
    return jnp.clip(result, min=-most, max=most).astype(kind)


def setup_inputs(seed: int = 0) -> dict:
    key_of = jax.random.split(jax.random.key(seed), 19)
    features = noise(key_of[0], (IMAGES, MAP, MAP, C_IN), 1.0, 6.0, ((0, 8), (3, 4)))
    labels = with_ends(jax.random.randint(key_of[1], (IMAGES,), 0, CLASSES), jax.random.fold_in(key_of[1], 1), 0, CLASSES - 1).astype(jnp.int32)
    class_weights = with_ends(jax.random.randint(key_of[2], (CLASSES,), 1, 11), jax.random.fold_in(key_of[2], 1), 1, 10).astype(jnp.int32)
    conv_in = noise(key_of[3], (C_IN, MID), C_IN ** -0.5, 0.125, ((0, 8), (1, 4)), jnp.float32)
    conv_mid = noise(key_of[4], (3, 3, MID, MID), (9 * MID) ** -0.5, 0.09375, ((2, 8), (3, 4)), jnp.float32)
    conv_out = noise(key_of[5], (MID, C_IN), MID ** -0.5, 0.25, ((0, 4), (1, 8)), jnp.float32)
    classifier = draw_classifier(jax.random.fold_in(key_of[18], 71), 0)
    norms = draw_norms(jax.random.fold_in(key_of[18], 71), 0)
    momentum_in = noise(key_of[8], (C_IN, MID), 0.002, 0.03125, ((0, 8), (1, 4)), jnp.float32)
    momentum_mid = noise(key_of[9], (3, 3, MID, MID), 0.002, 0.03125, ((2, 8), (3, 4)), jnp.float32)
    momentum_out = noise(key_of[10], (MID, C_IN), 0.002, 0.03125, ((0, 4), (1, 8)), jnp.float32)
    momentum_head = noise(key_of[11], (C_IN, CLASSES), 0.002, 0.03125, ((0, 8), (1, 4)), jnp.float32)
    momentum_norms = noise(key_of[12], (2, N_CHAN, 2 * MID // N_CHAN + C_IN // N_CHAN), 0.003, 0.046875, ((1, 4),), jnp.float32)
    average_in = noise(key_of[13], (C_IN, MID), C_IN ** -0.5, 0.125, ((0, 8), (1, 4)), jnp.float32)
    average_mid = noise(key_of[14], (3, 3, MID, MID), (9 * MID) ** -0.5, 0.09375, ((2, 8), (3, 4)), jnp.float32)
    average_out = noise(key_of[15], (MID, C_IN), MID ** -0.5, 0.25, ((0, 4), (1, 8)), jnp.float32)
    average_head = noise(key_of[16], (C_IN, CLASSES), C_IN ** -0.5, 0.125, ((0, 8), (1, 4)), jnp.float32)
    average_norms = jnp.clip(1.0 + 0.1 * jax.random.normal(key_of[17], (2, N_CHAN, 2 * MID // N_CHAN + C_IN // N_CHAN), jnp.float32), 0.5, 1.5)
    return {"features": features, "labels": labels, "class_weights": class_weights, "conv_in": conv_in, "conv_mid": conv_mid, "conv_out": conv_out, "classifier": classifier, "norms": norms, "momentum_in": momentum_in, "momentum_mid": momentum_mid, "momentum_out": momentum_out, "momentum_head": momentum_head, "momentum_norms": momentum_norms, "average_in": average_in, "average_mid": average_mid, "average_out": average_out, "average_head": average_head, "average_norms": average_norms}


HIGH = lax.Precision.HIGHEST
EPS = 1e-05
MOMENTUM = 0.5
AVERAGE = 0.5
RATE_MATRIX = 16.0
RATE_NORM = 64.0

@jax.custom_vjp
def low(v):
    return lax.optimization_barrier(v.astype(jnp.bfloat16)).astype(jnp.float32)

@jax.custom_vjp
def low_back(v):
    return v

def low_keep(v):
    return (low(v), None)

def low_pass(kept, grad):
    return (grad,)

def back_keep(v):
    return (v, None)

def back_low(kept, grad):
    return (low(grad),)
low.defvjp(low_keep, low_pass)
low_back.defvjp(back_keep, back_low)

def batch_norm(hidden, gain, shift):
    mean = lax.optimization_barrier(jnp.mean(hidden, axis=(0, 1, 2)))
    square = lax.optimization_barrier(jnp.mean(hidden * hidden, axis=(0, 1, 2)))
    return (hidden - mean) * lax.rsqrt(square - mean * mean + EPS) * gain + shift

def spatial(inputs, kernel):
    size = inputs.shape[1]
    padded = jnp.pad(inputs, ((0, 0), (1, 1), (1, 1), (0, 0)))
    total = jnp.zeros(inputs.shape[:3] + (kernel.shape[3],), jnp.float32)
    for row in range(3):
        for col in range(3):
            window = padded[:, row:row + size, col:col + size, :]
            total = total + jnp.einsum('bhwc,cd->bhwd', window, kernel[row, col], precision=HIGH)
    return total

def columns(table, start, stop):
    return table[:, start:stop].reshape(-1)

def loss_terms(params, inputs, labels, weight_row):
    conv_in, conv_mid, conv_out, classifier, norms = params
    narrow = MID // N_CHAN
    gains = norms[0]
    shifts = norms[1]
    gain_one, shift_one = (columns(gains, 0, narrow), columns(shifts, 0, narrow))
    gain_two, shift_two = (columns(gains, narrow, 2 * narrow), columns(shifts, narrow, 2 * narrow))
    gain_three, shift_three = (columns(gains, 2 * narrow, gains.shape[1]), columns(shifts, 2 * narrow, gains.shape[1]))
    hidden_one = low_back(jnp.einsum('bhwc,cd->bhwd', inputs, low(conv_in), precision=HIGH))
    act_one = low(jax.nn.silu(batch_norm(hidden_one, gain_one, shift_one)))
    hidden_two = low_back(spatial(act_one, low(conv_mid)))
    act_two = low(jax.nn.silu(batch_norm(hidden_two, gain_two, shift_two)))
    hidden_three = low_back(jnp.einsum('bhwc,cd->bhwd', act_two, low(conv_out), precision=HIGH))
    output = jax.nn.silu(batch_norm(hidden_three, gain_three, shift_three) + inputs)
    pooled = low(lax.optimization_barrier(jnp.mean(output, axis=(1, 2))))
    logits = low_back(jnp.dot(pooled, low(classifier), precision=HIGH))
    top = lax.optimization_barrier(jnp.max(logits, axis=1, keepdims=True))
    spread = top[:, 0] + jnp.log(lax.optimization_barrier(jnp.sum(jnp.exp(logits - top), axis=1)))
    picked = jnp.take_along_axis(logits, labels[:, None].astype(jnp.int32), axis=1)[:, 0]
    return jnp.sum(weight_row * (spread - picked))

def advance(weight, grad, momentum, average, rate):
    fresh = MOMENTUM * momentum + grad
    weight_new = weight - rate * (grad + MOMENTUM * fresh)
    return (weight_new, fresh, AVERAGE * average + (1.0 - AVERAGE) * weight_new)

def reference(features, labels, class_weights, conv_in, conv_mid, conv_out, classifier, norms, momentum_in, momentum_mid, momentum_out, momentum_head, momentum_norms, average_in, average_mid, average_out, average_head, average_norms):
    inputs = features.astype(jnp.float32)
    weight_row = class_weights[labels].astype(jnp.float32)
    weight_sum = jnp.sum(weight_row)
    params = (conv_in, conv_mid, conv_out, classifier, norms)
    loss_sum, pullback = jax.vjp(lambda p: loss_terms(p, inputs, labels, weight_row), params)
    grads = pullback(1.0 / weight_sum)[0]
    moments = (momentum_in, momentum_mid, momentum_out, momentum_head, momentum_norms)
    averages = (average_in, average_mid, average_out, average_head, average_norms)
    rates = (RATE_MATRIX, RATE_MATRIX, RATE_MATRIX, RATE_MATRIX, RATE_NORM)
    results = [advance(p, g, m, a, r) for p, g, m, a, r in zip(params, grads, moments, averages, rates)]
    news = [item[0] for item in results]
    freshs = [item[1] for item in results]
    means = [item[2] for item in results]
    copies = [item.astype(jnp.bfloat16) for item in news]
    return (loss_sum, weight_sum, news[0], news[1], news[2], news[3], news[4], freshs[0], freshs[1], freshs[2], freshs[3], freshs[4], means[0], means[1], means[2], means[3], means[4], copies[0], copies[1], copies[2], copies[3], copies[4])
```

```python
import functools

import jax
import jax.numpy as jnp
from jax import lax
from jax.experimental import pallas as pl
from jax.experimental.pallas import tpu as pltpu
from jax.sharding import PartitionSpec as P

EPS = 1e-05
MOMENTUM = 0.5
AVERAGE = 0.5
RATE_MATRIX = 16.0
RATE_NORM = 64.0
AXES = ("dp", "chan")
F32 = jnp.float32
BF16 = jnp.bfloat16
CHUNK = 80
LANES = 128


def swap(array, mask, n):
    return lax.ppermute(array, AXES, [(d, d ^ mask) for d in range(n)])


def tree_sum(parts):
    while len(parts) > 1:
        parts = [parts[k] + parts[k + 1] for k in range(0, len(parts), 2)]
    return parts[0]


def high_masks(n):
    return [8 * k for k in range(n // 8)]


def total(array, n):
    array = array + swap(array, 1, n)
    array = tree_sum([array] + [swap(array, mask, n) for mask in (2, 4, 6)])
    return tree_sum([array] + [swap(array, mask, n) for mask in high_masks(n)[1:]])


def gather(shard, n):
    stack = jnp.stack([shard] + [swap(shard, mask, n) for mask in high_masks(n)[1:]])
    even = [stack] + [swap(stack, mask, n) for mask in (2, 4, 6)]
    odd = [swap(part, 1, n) for part in even]
    return [even[0], odd[0], even[1], odd[1], even[2], odd[2], even[3], odd[3]]


def scatter_sum(parts, n):
    arrived = [swap(parts[k], 1, n) for k in (3, 5, 7, 1)]
    merged = [
        (own.astype(F32) + other.astype(F32)).astype(BF16)
        for own, other in zip((parts[2], parts[4], parts[6], parts[0]), arrived)
    ]
    across = [swap(merged[k], 2 * k + 2, n) for k in range(3)]
    both = tree_sum([part.astype(F32) for part in [merged[3]] + across]).astype(BF16)
    last = [both[0]] + [swap(both[a], mask, n) for a, mask in enumerate(high_masks(n)) if a]
    return tree_sum([part.astype(F32) for part in last])


def call(kernel, outs, *inputs, flops=0):
    moved = sum(x.size * x.dtype.itemsize for x in inputs)
    shapes = [jax.ShapeDtypeStruct(*out) for out in outs]
    moved += sum(s.size * s.dtype.itemsize for s in shapes)
    return pl.pallas_call(
        kernel,
        out_shape=shapes,
        in_specs=[pl.BlockSpec(memory_space=pltpu.SMEM)]
        + [pl.BlockSpec(memory_space=pltpu.VMEM)] * (len(inputs) - 1),
        out_specs=[pl.BlockSpec(memory_space=pltpu.VMEM)] * len(outs),
        compiler_params=pltpu.CompilerParams(vmem_limit_bytes=56 * 2**20),
        cost_estimate=pl.CostEstimate(flops=flops, bytes_accessed=moved, transcendentals=0),
    )(*inputs)


def sigmoid(value):
    return 0.5 * jnp.tanh(0.5 * value) + 0.5


def silu_grad(value):
    sigma = sigmoid(value)
    return sigma * (1.0 + value * (1.0 - sigma))


def dot(a, b, dims=((1,), (0,))):
    return lax.dot_general(a, b, (dims, ((), ())), preferred_element_type=F32)


def statistics(sums_ref, count, cols):
    mean = sums_ref[0:1, cols] / count
    square = sums_ref[1:2, cols] / count
    return mean, lax.rsqrt(square - mean * mean + EPS)


def col_sum(value):
    return jnp.sum(value, axis=0, keepdims=True)


def rows_of(step):
    return pl.ds(pl.multiple_of(step * CHUNK, CHUNK), CHUNK)


def assemble_kernel(c, *refs):
    me, *parts, out = refs
    number = me[0] * c + me[1]
    for k, part in enumerate(parts):
        for a in range(part.shape[0]):
            other = number ^ (8 * a + k)
            i, j = lax.div(other, c), lax.rem(other, c)
            if len(out.shape) == 3:
                rows, cols = part.shape[2:]
                out[
                    :,
                    pl.ds(pl.multiple_of(i * rows, rows), rows),
                    pl.ds(pl.multiple_of(j * cols, cols), cols),
                ] = part[a]
            else:
                rows, cols = part.shape[1:]
                out[
                    pl.ds(pl.multiple_of(i * rows, rows), rows),
                    pl.ds(pl.multiple_of(j * cols, cols), cols),
                ] = part[a]


def assemble_out_kernel(c, *refs):
    me, *parts, out = refs
    number = me[0] * c + me[1]
    for k, part in enumerate(parts):
        for a in range(part.shape[0]):
            other = number ^ (8 * a + k)
            i, j = lax.div(other, c), lax.rem(other, c)
            rows, cols = part.shape[1:]
            out[
                pl.ds(pl.multiple_of(j * rows, rows), rows),
                pl.ds(pl.multiple_of(i * cols, cols), cols),
            ] = part[a]


def first_kernel(me, weight_sum, *refs):
    *features, weights, hidden, sums = refs
    chan, depth = me[1], features[0].shape[1]
    width = hidden.shape[1]
    for start in range(0, width, 256):
        cols = slice(start, start + 256)
        value = None
        for k, part in enumerate(features):
            rows = pl.ds(pl.multiple_of((chan ^ k) * depth, depth), depth)
            term = dot(part[...], weights[rows, cols])
            value = term if value is None else value + term
        hidden[:, cols] = value
        sums[0:1, cols] = col_sum(value)
        sums[1:2, cols] = col_sum(value * value)
    sums[2:3, :] = jnp.broadcast_to(weight_sum[...], (1, width))


def windows(pad, out, size, group):
    line = size * group
    rows, width = out.shape[0], pad.shape[2]
    for i in range(3):
        for j in range(3):
            tap = 3 * i + j
            out[:, tap * width : (tap + 1) * width] = pad[
                j, i * line : i * line + rows, :
            ].astype(BF16)


def fill(pad, size, group):
    line = size * group
    rows, width = pad.shape[1] - 2 * line, pad.shape[2]
    place = lax.broadcasted_iota(jnp.int32, (rows, 1), 0)
    column = lax.rem(lax.div(place, group), size)
    here = pad[1, line : line + rows, :]
    empty = jnp.zeros((line, width), F32)
    for j in (0, 2):
        moved = pltpu.roll(here, group if j == 0 else rows - group, 0)
        valid = column != (0 if j == 0 else size - 1)
        pad[j, 0:line, :] = empty
        pad[j, line : line + rows, :] = jnp.where(valid, moved, 0.0)
        pad[j, line + rows :, :] = empty


def second_kernel(count, size, group, me, hidden, sums, norms, weights, cols, out, out_sums, pad):
    rows, width = hidden.shape
    line = size * group
    mean, scale = statistics(sums, count, slice(None))
    gain, shift = norms[0:1, :], norms[1:2, :]
    pad[1, 0:line, :] = jnp.zeros((line, width), F32)
    pad[1, line + rows :, :] = jnp.zeros((line, width), F32)
    for step in range(rows // CHUNK):
        part = slice(step * CHUNK, (step + 1) * CHUNK)
        value = (hidden[part, :] - mean) * scale * gain + shift
        act = (value * sigmoid(value)).astype(BF16).astype(F32)
        pad[1, line + step * CHUNK : line + (step + 1) * CHUNK, :] = act
    fill(pad, size, group)
    windows(pad, cols, size, group)
    for start in range(0, out.shape[1], 256):
        block = slice(start, start + 256)
        value = dot(cols[...], weights[:, block])
        out[:, block] = value
        out_sums[0:1, block] = col_sum(value)
        out_sums[1:2, block] = col_sum(value * value)


def third_kernel(count, me, hidden, sums, norms, weights, act, out, out_sums):
    mean, scale = statistics(sums, count, slice(None))
    gain, shift = norms[0:1, :], norms[1:2, :]
    for step in range(hidden.shape[0] // CHUNK):
        part = slice(step * CHUNK, (step + 1) * CHUNK)
        value = (hidden[part, :] - mean) * scale * gain + shift
        act[part, :] = (value * sigmoid(value)).astype(BF16)
    for start in range(0, out.shape[1], 256):
        block = slice(start, start + 256)
        value = dot(act[...], weights[:, block])
        out[:, block] = value
        out_sums[0:1, block] = col_sum(value)
        out_sums[1:2, block] = col_sum(value * value)


def head_kernel(count, pixels, group, classes, me, hidden, sums, norms, row_weights, target, weights, *refs):
    *features, upper, out_sums, packed, loss = refs
    chan, rows = me[1], hidden.shape[0]
    width = features[0].shape[1]
    twice = 2 * group
    blocks = [pl.ds(pl.multiple_of((chan ^ k) * width, width), width) for k in range(len(features))]
    for k, cols in enumerate(blocks):
        mean, scale = statistics(sums, count, cols)
        gain = scale * norms[0:1, cols]
        shift = norms[1:2, cols] - mean * gain

        def forward(step, pool, k=k, cols=cols, gain=gain, shift=shift):
            part = rows_of(step)
            value = hidden[part, cols] * gain + shift + features[k][part, :].astype(F32)
            upper[part, cols] = value
            value = value * sigmoid(value)
            return pool + jnp.sum(value.reshape(CHUNK // twice, twice, width), axis=0)

        pool = lax.fori_loop(0, rows // CHUNK, forward, jnp.zeros((twice, width), F32))
        pool = (pool + pltpu.roll(pool, group, 0)) / pixels
        packed[:, cols] = pool.astype(BF16)
    depth, space = weights.shape
    pooled = packed[:, 0:depth]
    logits = dot(pooled, weights[...])
    column = lax.broadcasted_iota(jnp.int32, logits.shape, 1)
    valid = lax.rem(column, space // len(features)) < classes
    top = jnp.max(jnp.where(valid, logits, -jnp.inf), axis=1, keepdims=True)
    grown = jnp.where(valid, jnp.exp(logits - top), 0.0)
    spread = top + jnp.log(jnp.sum(grown, axis=1, keepdims=True))
    wanted = target[...]
    picked = jnp.sum(wanted * logits, axis=1, keepdims=True)
    weight, share = row_weights[:, 0:1], row_weights[:, 1:2]
    loss[...] = 0.5 * jnp.sum(weight * (spread - picked), axis=0, keepdims=True)
    down = share * (jnp.where(valid, jnp.exp(logits - spread), 0.0) - wanted)
    packed[:, depth:] = down.astype(BF16)
    low_down = down.astype(BF16)
    for k, cols in enumerate(blocks):
        mean, scale = statistics(sums, count, cols)
        back = dot(low_down, weights[cols, :], ((1,), (1,))) / pixels
        back = jnp.broadcast_to(back[None], (CHUNK // twice, twice, width)).reshape(CHUNK, width)

        def backward(step, so_far, cols=cols, mean=mean, scale=scale, back=back):
            part = rows_of(step)
            value = back * silu_grad(upper[part, cols])
            normed = (hidden[part, cols] - mean) * scale
            upper[part, cols] = value
            return (so_far[0] + col_sum(value), so_far[1] + col_sum(value * normed))

        zero = jnp.zeros((1, width), F32)
        first, second = lax.fori_loop(0, rows // CHUNK, backward, (zero, zero))
        out_sums[0:1, cols] = first
        out_sums[1:2, cols] = second
    out_sums[2:3, :] = jnp.broadcast_to(loss[...], (1, out_sums.shape[1]))


def lower(upper, hidden, sums, back_sums, norms, count, part, cols):
    mean, scale = statistics(sums, count, cols)
    normed = (hidden[part, cols] - mean) * scale
    slope = scale * norms[0:1, cols]
    return slope * (
        upper[part, cols] - back_sums[0:1, cols] / count - normed * (back_sums[1:2, cols] / count)
    )


def back_three_kernel(
    count, me, upper, hidden, sums, norms, back_sums, weights, hidden_two, sums_two, norms_two, down, out, out_sums
):
    rows, wide = upper.shape
    for start in range(0, wide, 512):
        cols = slice(start, start + 512)
        for step in range(rows // CHUNK):
            part = slice(step * CHUNK, (step + 1) * CHUNK)
            down[part, cols] = lower(
                upper, hidden, sums, back_sums, norms, count, part, cols
            ).astype(BF16)
    for start in range(0, out.shape[1], 256):
        cols = slice(start, start + 256)
        value = dot(down[...], weights[cols, :], ((1,), (1,)))
        finish(value, hidden_two, sums_two, norms_two, count, cols, out, out_sums)


def finish(value, hidden, sums, norms, count, cols, out, out_sums):
    mean, scale = statistics(sums, count, cols)
    normed = (hidden[:, cols] - mean) * scale
    value = value * silu_grad(normed * norms[0:1, cols] + norms[1:2, cols])
    out[:, cols] = value
    out_sums[0:1, cols] = col_sum(value)
    out_sums[1:2, cols] = col_sum(value * normed)


def back_two_kernel(
    count, size, group, me, upper, hidden, sums, norms, back_sums, weights, hidden_one, sums_one, norms_one,
    down, out, out_sums, pad, cols,
):
    rows, width = upper.shape
    line = size * group
    pad[1, 0:line, :] = jnp.zeros((line, width), F32)
    pad[1, line + rows :, :] = jnp.zeros((line, width), F32)
    for step in range(rows // CHUNK):
        part = slice(step * CHUNK, (step + 1) * CHUNK)
        value = lower(upper, hidden, sums, back_sums, norms, count, part, slice(None)).astype(BF16)
        down[part, :] = value
        pad[1, line + step * CHUNK : line + (step + 1) * CHUNK, :] = value.astype(F32)
    fill(pad, size, group)
    windows(pad, cols, size, group)
    for start in range(0, out.shape[1], 256):
        block = slice(start, start + 256)
        value = None
        for tap in range(9):
            base = (8 - tap) * out.shape[1] + start
            term = dot(
                cols[:, tap * width : (tap + 1) * width],
                weights[base : base + 256, :],
                ((1,), (1,)),
            )
            value = term if value is None else value + term
        finish(value, hidden_one, sums_one, norms_one, count, block, out, out_sums)


def spread_blocks(number, c, outs, block):
    for k, out in enumerate(outs):
        for a in range(out.shape[0]):
            other = number ^ (8 * a + k)
            out[a] = block(lax.div(other, c), lax.rem(other, c))


def at(index, size):
    return pl.ds(pl.multiple_of(index * size, size), size)


def grad_out_kernel(c, me, act, down, *refs):
    *outs, whole = refs
    for start in range(0, whole.shape[1], 512):
        cols = slice(start, start + 512)
        whole[:, cols] = dot(act[...], down[:, cols], ((0,), (0,))).astype(BF16)
    rows, width = outs[0].shape[1:]
    spread_blocks(
        me[0] * c + me[1], c, outs, lambda i, j: whole[at(j, rows), at(i, width)]
    )


def grad_mid_kernel(c, me, cols, down, *refs):
    *outs, whole = refs
    depth = whole.shape[1]
    for tap in range(9):
        whole[tap] = dot(
            cols[:, tap * depth : (tap + 1) * depth], down[...], ((0,), (0,))
        ).astype(BF16)
    rows, width = outs[0].shape[2:]
    spread_blocks(
        me[0] * c + me[1], c, outs, lambda i, j: whole[:, at(i, rows), at(j, width)]
    )


def grad_in_kernel(count, c, me, upper, hidden, sums, norms, back_sums, *refs):
    features, outs, whole, down = refs[:c], refs[c:-2], refs[-2], refs[-1]
    rows = upper.shape[0]
    for step in range(rows // CHUNK):
        part = slice(step * CHUNK, (step + 1) * CHUNK)
        down[part, :] = lower(
            upper, hidden, sums, back_sums, norms, count, part, slice(None)
        ).astype(BF16)
    depth = features[0].shape[1]
    for k, part in enumerate(features):
        whole[at(me[1] ^ k, depth), :] = dot(part[...], down[...], ((0,), (0,))).astype(BF16)
    height, width = outs[0].shape[1:]
    spread_blocks(
        me[0] * c + me[1], c, outs, lambda i, j: whole[at(i, height), at(j, width)]
    )


def call_with_scratch(kernel, outs, scratch, *inputs, flops=0):
    moved = sum(x.size * x.dtype.itemsize for x in inputs)
    shapes = [jax.ShapeDtypeStruct(*out) for out in outs]
    moved += sum(s.size * s.dtype.itemsize for s in shapes)
    return pl.pallas_call(
        kernel,
        out_shape=shapes,
        in_specs=[pl.BlockSpec(memory_space=pltpu.SMEM)]
        + [pl.BlockSpec(memory_space=pltpu.VMEM)] * (len(inputs) - 1),
        out_specs=[pl.BlockSpec(memory_space=pltpu.VMEM)] * len(outs),
        scratch_shapes=[pltpu.VMEM(*one) for one in scratch],
        compiler_params=pltpu.CompilerParams(vmem_limit_bytes=56 * 2**20),
        cost_estimate=pl.CostEstimate(flops=flops, bytes_accessed=moved, transcendentals=0),
    )(*inputs)


def advance(weight, grad, momentum, average, rate):
    fresh = MOMENTUM * momentum + grad
    weight_new = weight - rate * (grad + MOMENTUM * fresh)
    return (weight_new, fresh, AVERAGE * average + (1.0 - AVERAGE) * weight_new)


def ordered(parts, number, n):
    stacked = jnp.stack(parts, axis=1)
    stacked = stacked.reshape((n,) + parts[0].shape[1:])
    return jnp.take(stacked, jnp.arange(n) ^ number, axis=0)


def relative(blocks, number, n):
    blocks = jnp.take(blocks, jnp.arange(n) ^ number, axis=0)
    blocks = blocks.reshape((n // 8, 8) + blocks.shape[1:])
    return [blocks[:, k] for k in range(8)]


def shards(
    d,
    c,
    features,
    labels,
    class_weights,
    conv_in,
    conv_mid,
    conv_out,
    classifier,
    norms,
    momentum_in,
    momentum_mid,
    momentum_out,
    momentum_head,
    momentum_norms,
    average_in,
    average_mid,
    average_out,
    average_head,
    average_norms,
):
    n = d * c
    dp, chan = lax.axis_index("dp"), lax.axis_index("chan")
    number = dp * c + chan
    me = jnp.stack([dp, chan]).astype(jnp.int32)
    images, size = features.shape[0], features.shape[1]
    group = images // c
    pixels = size * size
    count = float(images * pixels * d)
    rows = pixels * group
    deep = features.shape[3]
    mid, wide = conv_in.shape[1] * c, deep * c
    aligned = conv_out.shape[1] % LANES == 0

    laid = features.transpose(1, 2, 0, 3).reshape(pixels, c, group, deep)
    laid = laid.transpose(1, 0, 2, 3).reshape(c, rows, deep)
    pieces = [lax.dynamic_index_in_dim(laid, chan ^ k, 0, keepdims=False) for k in range(c)]
    pieces = [pieces[0]] + [swap(pieces[k], k, n) for k in range(1, c)]

    low_in = gather(conv_in.astype(BF16), n)
    fan_in, fan_out = conv_mid.shape[2:]
    low_mid = gather(conv_mid.astype(BF16).reshape(9, fan_in, fan_out), n)
    low_out = gather(conv_out.astype(BF16), n)
    classes = classifier.shape[1]
    space = -(-classes // LANES) * LANES
    low_head = gather(jnp.pad(classifier.astype(BF16), ((0, 0), (0, space - classes))), n)

    table = norms[:, 0]
    tables = jnp.stack([table] + [swap(table, k, n) for k in range(1, c)])
    tables = jnp.take(tables, jnp.arange(c) ^ chan, axis=0).transpose(1, 0, 2)
    narrow = conv_in.shape[1]
    norms_one = tables[:, :, :narrow].reshape(2, mid)
    norms_two = tables[:, :, narrow : 2 * narrow].reshape(2, mid)
    norms_three = tables[:, :, 2 * narrow :].reshape(2, wide)

    own = lax.dynamic_index_in_dim(labels.reshape(c, group), chan, 0, keepdims=False)
    own = jnp.concatenate([own, own])
    catalog = lax.broadcasted_iota(jnp.int32, (2 * group, class_weights.shape[0]), 1)
    chosen = catalog == own[:, None]
    weight_row = jnp.sum(jnp.where(chosen, class_weights[None, :], 0), axis=1).astype(F32)
    target = jnp.pad(
        chosen.astype(F32).reshape(2 * group, c, classes), ((0, 0), (0, 0), (0, space - classes))
    ).reshape(2 * group, c * space)
    own_weight = (0.5 * jnp.sum(weight_row)).reshape(1, 1)

    def assembled(parts, shape, kernel):
        if aligned:
            return call(functools.partial(kernel, c), [(shape, BF16)], me, *parts)[0]
        blocks = ordered(parts, number, n)
        blocks = blocks.reshape((d, c) + blocks.shape[1:])
        if kernel is assemble_out_kernel:
            return blocks.transpose(1, 2, 0, 3).reshape(shape)
        if len(shape) == 3:
            return blocks.transpose(2, 0, 3, 1, 4).reshape(shape)
        return blocks.transpose(0, 2, 1, 3).reshape(shape)

    whole_in = assembled(low_in, (wide, mid), assemble_kernel)
    hidden_one, sums_one = call(
        first_kernel, [((rows, mid), F32), ((3, mid), F32)], me, own_weight, *pieces, whole_in,
        flops=2 * rows * wide * mid,
    )
    sums_one = total(sums_one, n)
    weight_sum = sums_one[2, 0]

    whole_mid = assembled(low_mid, (9, mid, mid), assemble_kernel).reshape(9 * mid, mid)
    line = size * group
    padded = ((3, rows + 2 * line, mid), F32)
    cols, hidden_two, sums_two = call_with_scratch(
        functools.partial(second_kernel, count, size, group),
        [((rows, 9 * mid), BF16), ((rows, mid), F32), ((2, mid), F32)],
        [padded],
        me, hidden_one, sums_one, norms_one, whole_mid,
        flops=18 * rows * mid * mid,
    )
    sums_two = total(sums_two, n)

    whole_out = assembled(low_out, (mid, wide), assemble_out_kernel)
    act_two, hidden_three, sums_three = call(
        functools.partial(third_kernel, count),
        [((rows, mid), BF16), ((rows, wide), F32), ((2, wide), F32)],
        me, hidden_two, sums_two, norms_two, whole_out,
        flops=2 * rows * mid * wide,
    )
    sums_three = total(sums_three, n)

    whole_head = assembled(low_head, (wide, c * space), assemble_kernel)
    row_weights = jnp.stack([weight_row, weight_row / weight_sum], axis=1)
    upper_three, back_three, packed, _ = call(
        functools.partial(head_kernel, count, pixels, group, classes),
        [((rows, wide), F32), ((3, wide), F32), ((2 * group, wide + c * space), BF16), ((1, 1), F32)],
        me, hidden_three, sums_three, norms_three, row_weights, target, whole_head, *pieces,
        flops=4 * 8 * wide * c * space,
    )
    everything = lax.all_gather(packed[:group], AXES, axis=0, tiled=True)
    back_three = total(back_three, n)
    loss_sum = back_three[2, 0]

    down_three, upper_two, back_two = call(
        functools.partial(back_three_kernel, count),
        [((rows, wide), BF16), ((rows, mid), F32), ((2, mid), F32)],
        me, upper_three, hidden_three, sums_three, norms_three, back_three, whole_out,
        hidden_two, sums_two, norms_two,
        flops=2 * rows * mid * wide,
    )
    back_two = total(back_two, n)

    def blocks_of(shape):
        return [((n // 8,) + shape, BF16)] * 8

    if aligned:
        parts_out = call_with_scratch(
            functools.partial(grad_out_kernel, c), blocks_of(conv_out.shape), [((mid, wide), BF16)],
            me, act_two, down_three, flops=2 * rows * mid * wide,
        )
    else:
        whole = dot(act_two, down_three, ((0,), (0,))).astype(BF16)
        whole = whole.reshape((c, conv_out.shape[0], d, conv_out.shape[1])).transpose(2, 0, 1, 3)
        parts_out = relative(whole.reshape((n,) + conv_out.shape), number, n)
    grad_out = scatter_sum(parts_out, n)

    down_two, upper_one, back_one = call_with_scratch(
        functools.partial(back_two_kernel, count, size, group),
        [((rows, mid), BF16), ((rows, mid), F32), ((2, mid), F32)],
        [padded, ((rows, 9 * mid), BF16)],
        me, upper_two, hidden_two, sums_two, norms_two, back_two, whole_mid,
        hidden_one, sums_one, norms_one,
        flops=18 * rows * mid * mid,
    )
    back_one = total(back_one, n)

    shard_mid = (9, fan_in, fan_out)
    parts_mid = call_with_scratch(
        functools.partial(grad_mid_kernel, c), blocks_of(shard_mid), [((9, mid, mid), BF16)],
        me, cols, down_two, flops=18 * rows * mid * mid,
    )
    grad_mid = scatter_sum(parts_mid, n).reshape(conv_mid.shape)

    parts_in = call_with_scratch(
        functools.partial(grad_in_kernel, count, c), blocks_of(conv_in.shape),
        [((wide, mid), BF16), ((rows, mid), BF16)],
        me, upper_one, hidden_one, sums_one, norms_one, back_one, *pieces,
        flops=2 * rows * mid * wide,
    )
    grad_in = scatter_sum(parts_in, n)

    height = classifier.shape[0]
    pooled = lax.dynamic_slice_in_dim(everything, dp * height, height, axis=1)
    upper_logits = lax.dynamic_slice_in_dim(everything, wide + chan * space, space, axis=1)
    grad_head = dot(pooled, upper_logits, ((0,), (0,)))[:, :classes]

    def mine(sums, width):
        return lax.dynamic_slice_in_dim(sums[:2], chan * width, width, axis=1)[::-1]

    grad_norms = jnp.concatenate(
        [mine(back_one, narrow), mine(back_two, narrow), mine(back_three, deep)], axis=1
    )[:, None, :]
    params = (conv_in, conv_mid, conv_out, classifier, norms)
    grads = (grad_in, grad_mid, grad_out, grad_head, grad_norms)
    moments = (momentum_in, momentum_mid, momentum_out, momentum_head, momentum_norms)
    averages = (average_in, average_mid, average_out, average_head, average_norms)
    rates = (RATE_MATRIX, RATE_MATRIX, RATE_MATRIX, RATE_MATRIX, RATE_NORM)
    results = [
        advance(p, g, m, a, r) for p, g, m, a, r in zip(params, grads, moments, averages, rates)
    ]
    news = [item[0] for item in results]
    freshs = [item[1] for item in results]
    means = [item[2] for item in results]
    copies = [item.astype(BF16) for item in news]
    return (loss_sum, weight_sum, *news, *freshs, *means, *copies)


def solution(mesh):
    matrices = (P("dp", "chan"), P(None, None, "dp", "chan"), P("chan", "dp"), P("dp", "chan"), P(None, "chan", None))
    return jax.shard_map(
        functools.partial(shards, mesh.shape["dp"], mesh.shape["chan"]),
        mesh=mesh,
        in_specs=(P("dp", None, None, "chan"), P("dp"), P()) + matrices * 3,
        out_specs=(P(), P()) + matrices * 4,
        check_vma=False,
    )
```

```python
import functools
import math

import jax
import jax.numpy as jnp
from jax import lax
from jax.experimental import pallas as pl
from jax.experimental.pallas import tpu as pltpu
from jax.sharding import PartitionSpec as P

EPS = 1e-05
MOMENTUM = 0.5
AVERAGE = 0.5
RATE_MATRIX = 16.0
RATE_NORM = 64.0
AXES = ("dp", "chan")
F32 = jnp.float32
BF16 = jnp.bfloat16
CHUNK = 80
LANES = 128


def swap(array, mask, n):
    return lax.ppermute(array, AXES, [(d, d ^ mask) for d in range(n)])


def tree_sum(parts):
    while len(parts) > 1:
        parts = [parts[k] + parts[k + 1] for k in range(0, len(parts), 2)]
    return parts[0]


def high_masks(n):
    return [8 * k for k in range(n // 8)]


def total(array, n, early=None, late=None):
    pair = following(array + swap(array, 1, n), early)
    array = tree_sum([pair] + [swap(pair, mask, n) for mask in (2, 4, 6)])
    array = following(array, late)
    return tree_sum([array] + [swap(array, mask, n) for mask in high_masks(n)[1:]]), array, pair


def following(value, earlier):
    return value if earlier is None else lax.optimization_barrier((value, earlier))[0]


def gather_high(shard, n):
    return [shard] + [swap(shard, mask, n) for mask in high_masks(n)[1:]]


def gather_low(parts, halves, n, after=None):
    stack, masks = following(jnp.stack(parts), after), high_masks(n)
    near, side = swap(stack, 2, n), swap(stack, 4, n)
    half = len(masks) // 2
    pairs = [(stack, masks), (side, [m ^ 4 for m in masks]), (near, [m ^ 2 for m in masks])]
    if halves:
        pairs.append((swap(near[:half], 4, n), [m ^ 6 for m in masks[:half]]))
        pairs.append((swap(side[half:], 2, n), [m ^ 6 for m in masks[half:]]))
    else:
        pairs.append((swap(stack, 6, n), [m ^ 6 for m in masks]))
    pairs += [(swap(array, 1, n), [m ^ 1 for m in row]) for array, row in pairs]
    return pairs, side


def slot_masks(n):
    return [[core ^ low ^ high for low in (0, 2, 4, 6) for high in high_masks(n)] for core in (0, 1)]


def scatter_start(own, other, n):
    outs = [((n // 8,) + own.shape[1:], BF16)] * 4
    return call(add_first_kernel, outs, swap(other, 1, n), own, anywhere=True)


def scatter_next(kept, arrived, n):
    shape = kept.shape[1:]
    outs = [(shape, F32)] + [(shape, BF16)] * (n // 8 - 1)
    return call(add_next_kernel, outs, kept, *arrived, anywhere=True)


def scatter_last(sums, n):
    return [sums[0]] + [swap(part, mask, n) for part, mask in zip(sums[1:], high_masks(n)[1:])]


def added(parts):
    return tree_sum([part.astype(F32) for part in parts])


def call(kernel, outs, *inputs, flops=0, anywhere=False, scratch=(), semaphores=(), space=pltpu.VMEM):
    moved = sum(x.size * x.dtype.itemsize for x in inputs)
    shapes = [jax.ShapeDtypeStruct(*out) for out in outs]
    moved += sum(s.size * s.dtype.itemsize for s in shapes)
    held = sum(math.prod(shape) * dtype(0).itemsize for shape, dtype in scratch)
    specs = [pl.BlockSpec(memory_space=space)] * len(inputs)
    if not anywhere:
        specs[0] = pl.BlockSpec(memory_space=pltpu.SMEM)
    return pl.pallas_call(
        kernel,
        out_shape=shapes,
        in_specs=specs,
        out_specs=[pl.BlockSpec(memory_space=pltpu.VMEM)] * len(outs),
        scratch_shapes=[pltpu.VMEM(*one) for one in scratch] + list(semaphores),
        compiler_params=pltpu.CompilerParams(vmem_limit_bytes=max(moved // 2, 8 * 2**20) + held + 4 * 2**20),
        cost_estimate=pl.CostEstimate(flops=flops, bytes_accessed=moved, transcendentals=0),
    )(*inputs)


def sigmoid(value):
    return 0.5 * jnp.tanh(0.5 * value) + 0.5


def silu_grad(value):
    sigma = sigmoid(value)
    return sigma * (1.0 + value * (1.0 - sigma))


def dot(a, b, dims=((1,), (0,))):
    return lax.dot_general(a, b, (dims, ((), ())), preferred_element_type=F32)


def statistics(sums_ref, count, cols):
    mean = sums_ref[0:1, cols] / count
    square = sums_ref[1:2, cols] / count
    return mean, lax.rsqrt(square - mean * mean + EPS)


def col_sum(value):
    return jnp.sum(value, axis=0, keepdims=True)


def octet_sum(value):
    return jnp.sum(value.reshape(value.shape[0] // 8, 8, value.shape[1]), axis=0)


def rows_of(step):
    return pl.ds(pl.multiple_of(step * CHUNK, CHUNK), CHUNK)


def at(index, size):
    if isinstance(index, int):
        return pl.ds(index * size, size)
    return pl.ds(pl.multiple_of(index * size, size), size)


def assemble_kernel(c, plan, tall, me, *refs):
    *parts, out = refs
    number = me[0] * c + me[1]
    for part, masks in zip(parts, plan):
        for a, mask in enumerate(masks):
            other = number ^ mask
            i, j = lax.div(other, c), lax.rem(other, c)
            rows, cols = part.shape[-2:]
            if len(out.shape) == 3:
                out[:, at(i, rows), at(j, cols)] = part[a]
            elif tall:
                out[at(i, rows), at(j, cols)] = part[a]
            else:
                out[at(j, rows), at(i, cols)] = part[a]


def assemble_head_kernel(c, me, rest, out):
    n = rest.shape[0]
    rows, cols = out.shape[0] // (n // c), out.shape[1] // c
    for a in range(n):
        for k in range(cols // LANES):
            part = rest[a, k * rows : (k + 1) * rows, :]
            out[at(a // c, rows), a % c * cols + k * LANES : a % c * cols + (k + 1) * LANES] = part


def prepare_kernel(c, me, *refs):
    sources, outs, held, arrived = refs[:5], refs[5:-6], refs[-6:-1], refs[-1]
    pieces, (low_in, low_mid, low_out, low_head) = outs[:c], outs[c:]
    features, conv_in, conv_mid, conv_out, classifier = held
    order = (1, 0, 2, 3, 4)
    copies = [pltpu.make_async_copy(sources[k], held[k], arrived.at[k]) for k in range(5)]
    for k in order:
        copies[k].start()
    copies[1].wait()
    low_in[...] = conv_in[...].astype(BF16)
    copies[0].wait()
    pixels, images, width = features.shape
    group = images // c
    for t in range(c):
        part = features[:, t * group : (t + 1) * group, :].astype(F32)
        part = part.reshape(pixels * group, width).astype(BF16)
        for k in range(c):

            @pl.when(me[1] == t ^ k)
            def _(part=part, k=k):
                pieces[k][...] = part

    copies[2].wait()
    low_mid[...] = conv_mid[...].astype(BF16)
    copies[3].wait()
    low_out[...] = conv_out[...].astype(BF16)
    copies[4].wait()
    tall, classes = classifier.shape
    for k, start in enumerate(range(0, classes, LANES)):
        stop = min(start + LANES, classes)
        rows = slice(k * tall, (k + 1) * tall)
        low_head[rows, 0 : stop - start] = classifier[:, start:stop].astype(BF16)
        if stop - start < LANES:
            low_head[rows, stop - start :] = jnp.zeros((tall, LANES - stop + start), BF16)


def first_kernel(me, carried, *refs):
    *features, weights, hidden, sums = refs
    chan, depth = me[1], features[0].shape[1]
    width = hidden.shape[1]
    for start in range(0, width, 256):
        cols = slice(start, start + 256)
        value = None
        for k, part in enumerate(features):
            rows = pl.ds(pl.multiple_of((chan ^ k) * depth, depth), depth)
            term = dot(part[...], weights[rows, cols])
            value = term if value is None else value + term
        hidden[:, cols] = value
        sums[0:1, cols] = col_sum(value)
        sums[1:2, cols] = col_sum(value * value)
    sums[2:, :] = carried[...]


def windows(pad, out, size, group):
    line = size * group
    rows, width = out.shape[0], pad.shape[2]
    for i in range(3):
        for j in range(3):
            tap = 3 * i + j
            out[:, tap * width : (tap + 1) * width] = pad[
                j, i * line : i * line + rows, :
            ].astype(BF16)


def fill(pad, size, group):
    line = size * group
    rows, width = pad.shape[1] - 2 * line, pad.shape[2]
    place = lax.broadcasted_iota(jnp.int32, (rows, 1), 0)
    column = lax.rem(lax.div(place, group), size)
    here = pad[1, line : line + rows, :]
    empty = jnp.zeros((line, width), F32)
    for j in (0, 2):
        moved = pltpu.roll(here, group if j == 0 else rows - group, 0)
        valid = column != (0 if j == 0 else size - 1)
        pad[j, 0:line, :] = empty
        pad[j, line : line + rows, :] = jnp.where(valid, moved, 0.0)
        pad[j, line + rows :, :] = empty


def second_kernel(count, size, group, me, hidden, sums, norms, weights, cols, out, out_sums, pad):
    rows, width = hidden.shape
    line = size * group
    mean, scale = statistics(sums, count, slice(None))
    gain, shift = norms[0:1, :], norms[1:2, :]
    pad[1, 0:line, :] = jnp.zeros((line, width), F32)
    pad[1, line + rows :, :] = jnp.zeros((line, width), F32)
    for step in range(rows // CHUNK):
        part = slice(step * CHUNK, (step + 1) * CHUNK)
        value = (hidden[part, :] - mean) * scale * gain + shift
        act = (value * sigmoid(value)).astype(BF16).astype(F32)
        pad[1, line + step * CHUNK : line + (step + 1) * CHUNK, :] = act
    fill(pad, size, group)
    windows(pad, cols, size, group)
    for start in range(0, out.shape[1], 256):
        block = slice(start, start + 256)
        value = dot(cols[...], weights[:, block])
        out[:, block] = value
        out_sums[0:1, block] = col_sum(value)
        out_sums[1:2, block] = col_sum(value * value)


def third_kernel(count, me, hidden, sums, norms, weights, act, out, out_sums):
    mean, scale = statistics(sums, count, slice(None))
    gain, shift = norms[0:1, :], norms[1:2, :]
    for step in range(hidden.shape[0] // CHUNK):
        part = slice(step * CHUNK, (step + 1) * CHUNK)
        value = (hidden[part, :] - mean) * scale * gain + shift
        act[part, :] = (value * sigmoid(value)).astype(BF16)
    for start in range(0, out.shape[1], 256):
        block = slice(start, start + 256)
        value = dot(act[...], weights[:, block])
        out[:, block] = value
        out_sums[0:1, block] = col_sum(value)
        out_sums[1:2, block] = col_sum(value * value)


def head_kernel(count, pixels, group, classes, me, hidden, sums, norms, row_weights, target, weights, *refs):
    *features, upper, out_sums, packed, loss = refs
    chan, rows = me[1], hidden.shape[0]
    width = features[0].shape[1]
    twice = 2 * group
    blocks = [pl.ds(pl.multiple_of((chan ^ k) * width, width), width) for k in range(len(features))]
    for k, cols in enumerate(blocks):
        mean, scale = statistics(sums, count, cols)
        gain = scale * norms[0:1, cols]
        shift = norms[1:2, cols] - mean * gain

        def forward(step, pool, k=k, cols=cols, gain=gain, shift=shift):
            part = rows_of(step)
            value = hidden[part, cols] * gain + shift + features[k][part, :].astype(F32)
            sigma = sigmoid(value)
            value = value * sigma
            upper[part, cols] = sigma + value - value * sigma
            return pool + jnp.sum(value.reshape(CHUNK // twice, twice, width), axis=0)

        pool = lax.fori_loop(0, rows // CHUNK, forward, jnp.zeros((twice, width), F32))
        pool = (pool + pltpu.roll(pool, group, 0)) / pixels
        packed[:, cols] = pool.astype(BF16)
    depth, space = weights.shape
    pooled = packed[:, 0:depth]
    logits = dot(pooled, weights[...])
    column = lax.broadcasted_iota(jnp.int32, logits.shape, 1)
    valid = lax.rem(column, space // len(features)) < classes
    top = jnp.max(jnp.where(valid, logits, -jnp.inf), axis=1, keepdims=True)
    grown = jnp.where(valid, jnp.exp(logits - top), 0.0)
    spread = top + jnp.log(jnp.sum(grown, axis=1, keepdims=True))
    wanted = target[...]
    picked = jnp.sum(wanted * logits, axis=1, keepdims=True)
    weight, share = row_weights[:, 0:1], row_weights[:, 1:2]
    loss[...] = 0.5 * jnp.sum(weight * (spread - picked), axis=0, keepdims=True)
    down = share * (jnp.where(valid, jnp.exp(logits - spread), 0.0) - wanted)
    packed[:, depth:] = down.astype(BF16)
    low_down = down.astype(BF16)
    for k, cols in enumerate(blocks):
        mean, scale = statistics(sums, count, cols)
        back = dot(low_down, weights[cols, :], ((1,), (1,))) / pixels
        back = jnp.broadcast_to(back[None], (CHUNK // twice, twice, width)).reshape(CHUNK, width)

        def backward(step, so_far, cols=cols, mean=mean, back=back):
            part = rows_of(step)
            value = back * upper[part, cols]
            moved = value * (hidden[part, cols] - mean)
            upper[part, cols] = value
            return (so_far[0] + octet_sum(value), so_far[1] + octet_sum(moved))

        zero = jnp.zeros((8, width), F32)
        first, second = lax.fori_loop(0, rows // CHUNK, backward, (zero, zero))
        out_sums[0:1, cols] = col_sum(first)
        out_sums[1:2, cols] = col_sum(second) * scale
    out_sums[2:3, :] = jnp.broadcast_to(loss[...], (1, out_sums.shape[1]))


def lower(upper, hidden, sums, back_sums, norms, count, part, cols):
    mean, scale = statistics(sums, count, cols)
    normed = (hidden[part, cols] - mean) * scale
    slope = scale * norms[0:1, cols]
    return slope * (
        upper[part, cols] - back_sums[0:1, cols] / count - normed * (back_sums[1:2, cols] / count)
    )


def back_three_kernel(
    count, me, upper, hidden, sums, norms, back_sums, weights, hidden_two, sums_two, norms_two, down, out, out_sums
):
    rows, wide = upper.shape
    for start in range(0, wide, 512):
        cols = slice(start, start + 512)
        for step in range(rows // CHUNK):
            part = slice(step * CHUNK, (step + 1) * CHUNK)
            down[part, cols] = lower(
                upper, hidden, sums, back_sums, norms, count, part, cols
            ).astype(BF16)
    for start in range(0, out.shape[1], 256):
        cols = slice(start, start + 256)
        value = dot(down[...], weights[cols, :], ((1,), (1,)))
        finish(value, hidden_two, sums_two, norms_two, count, cols, out, out_sums)


def finish(value, hidden, sums, norms, count, cols, out, out_sums):
    mean, scale = statistics(sums, count, cols)
    normed = (hidden[:, cols] - mean) * scale
    value = value * silu_grad(normed * norms[0:1, cols] + norms[1:2, cols])
    out[:, cols] = value
    out_sums[0:1, cols] = col_sum(value)
    out_sums[1:2, cols] = col_sum(value * normed)


def back_two_kernel(
    count, size, group, me, upper, hidden, sums, norms, back_sums, weights, hidden_one, sums_one, norms_one,
    down, out, out_sums, pad, cols,
):
    rows, width = upper.shape
    line = size * group
    pad[1, 0:line, :] = jnp.zeros((line, width), F32)
    pad[1, line + rows :, :] = jnp.zeros((line, width), F32)
    for step in range(rows // CHUNK):
        part = slice(step * CHUNK, (step + 1) * CHUNK)
        value = lower(upper, hidden, sums, back_sums, norms, count, part, slice(None)).astype(BF16)
        down[part, :] = value
        pad[1, line + step * CHUNK : line + (step + 1) * CHUNK, :] = value.astype(F32)
    fill(pad, size, group)
    windows(pad, cols, size, group)
    for start in range(0, out.shape[1], 256):
        block = slice(start, start + 256)
        value = None
        for tap in range(9):
            base = (8 - tap) * out.shape[1] + start
            term = dot(
                cols[:, tap * width : (tap + 1) * width],
                weights[base : base + 256, :],
                ((1,), (1,)),
            )
            value = term if value is None else value + term
        finish(value, hidden_one, sums_one, norms_one, count, block, out, out_sums)


def spread_blocks(number, c, outs, masks, block):
    for out, row in zip(outs, masks):
        for a, mask in enumerate(row):
            other = number ^ mask
            out[a] = block(lax.div(other, c), lax.rem(other, c))


def grad_out_kernel(c, masks, me, act, down, *refs):
    *outs, whole = refs
    for start in range(0, whole.shape[1], 512):
        cols = slice(start, start + 512)
        whole[:, cols] = dot(act[...], down[:, cols], ((0,), (0,))).astype(BF16)
    rows, width = outs[0].shape[1:]
    spread_blocks(
        me[0] * c + me[1], c, outs, masks, lambda i, j: whole[at(j, rows), at(i, width)]
    )


def grad_mid_kernel(c, masks, me, cols, down, *refs):
    *outs, whole = refs
    depth = whole.shape[1]
    for tap in range(9):
        whole[tap] = dot(
            cols[:, tap * depth : (tap + 1) * depth], down[...], ((0,), (0,))
        ).astype(BF16)
    rows, width = outs[0].shape[2:]
    spread_blocks(
        me[0] * c + me[1], c, outs, masks, lambda i, j: whole[:, at(i, rows), at(j, width)]
    )


def grad_in_kernel(count, c, masks, me, upper, hidden, sums, norms, back_sums, *refs):
    features, outs, whole, down = refs[:c], refs[c:-2], refs[-2], refs[-1]
    rows = upper.shape[0]
    for step in range(rows // CHUNK):
        part = slice(step * CHUNK, (step + 1) * CHUNK)
        down[part, :] = lower(
            upper, hidden, sums, back_sums, norms, count, part, slice(None)
        ).astype(BF16)
    depth = features[0].shape[1]
    for k, part in enumerate(features):
        whole[at(me[1] ^ k, depth), :] = dot(part[...], down[...], ((0,), (0,))).astype(BF16)
    height, width = outs[0].shape[1:]
    spread_blocks(
        me[0] * c + me[1], c, outs, masks, lambda i, j: whole[at(i, height), at(j, width)]
    )


def add_low(one, other):
    return (one.astype(F32) + other.astype(F32)).astype(BF16)


def add_first_kernel(arrived, own, *outs):
    z = own.shape[0] // 4
    for low, out in enumerate(outs):
        for k in range(z):
            out[k] = add_low(own[low * z + k], arrived[low * z + k])


def add_next_kernel(kept, one, two, three, *outs):
    for k, out in enumerate(outs):
        pair = kept[k].astype(F32) + one[k].astype(F32)
        out[...] = (pair + (two[k].astype(F32) + three[k].astype(F32))).astype(out.dtype)


def advance(weight, grad, momentum, average, rate):
    fresh = MOMENTUM * momentum + grad
    weight_new = weight - rate * (grad + MOMENTUM * fresh)
    return (weight_new, fresh, AVERAGE * average + (1.0 - AVERAGE) * weight_new)


def shards(
    d,
    c,
    features,
    labels,
    class_weights,
    conv_in,
    conv_mid,
    conv_out,
    classifier,
    norms,
    momentum_in,
    momentum_mid,
    momentum_out,
    momentum_head,
    momentum_norms,
    average_in,
    average_mid,
    average_out,
    average_head,
    average_norms,
):
    n = d * c
    dp, chan = lax.axis_index("dp"), lax.axis_index("chan")
    number = dp * c + chan
    me = jnp.stack([dp, chan]).astype(jnp.int32)
    images, size = features.shape[0], features.shape[1]
    group = images // c
    pixels = size * size
    count = float(images * pixels * d)
    rows = pixels * group
    deep = features.shape[3]
    mid, wide = conv_in.shape[1] * c, deep * c
    aligned = conv_out.shape[1] % LANES == 0

    fan_in, fan_out = conv_mid.shape[2:]
    classes = classifier.shape[1]
    space = -(-classes // LANES) * LANES
    tall = classifier.shape[0]
    laid = features.transpose(1, 2, 0, 3).reshape(pixels, images, deep)
    narrow_mid = conv_mid.reshape(9, fan_in, fan_out)
    sources = (laid, conv_in, narrow_mid, conv_out, classifier)
    own, mate, other, away, low_in, low_mid, low_out, low_head = call(
        functools.partial(prepare_kernel, c),
        [((rows, deep), BF16)] * c
        + [(x.shape, BF16) for x in (conv_in, narrow_mid, conv_out)]
        + [((tall * (space // LANES), LANES), BF16)],
        me, *[pltpu.with_memory_space_constraint(x, pltpu.HBM) for x in sources], space=pltpu.HBM,
        scratch=[(x.shape, jnp.dtype(x.dtype).type) for x in sources],
        semaphores=[pltpu.SemaphoreType.DMA((5,))],
    )
    away, other = swap(away, 2, n), swap(other, 2, n)
    high_in = gather_high(low_in, n)
    low_head = lax.all_gather(low_head, AXES)
    pieces = [own, swap(mate, 1, n), other, swap(away, 1, n)]
    low_in, side_in = gather_low(high_in, False, n, (away, other))
    high_mid = gather_high(following(low_mid, high_in[1]), n)
    low_mid, _ = gather_low(high_mid, True, n, side_in)
    high_out = gather_high(following(low_out, high_mid[1]), n)

    narrow = conv_in.shape[1]
    own = lax.dynamic_index_in_dim(labels.reshape(c, group), chan, 0, keepdims=False)
    own = jnp.concatenate([own, own])
    catalog = lax.broadcasted_iota(jnp.int32, (2 * group, class_weights.shape[0]), 1)
    chosen = catalog == own[:, None]
    weight_row = jnp.sum(jnp.where(chosen, class_weights[None, :], 0), axis=1).astype(F32)
    target = jnp.pad(
        chosen.astype(F32).reshape(2 * group, c, classes), ((0, 0), (0, 0), (0, space - classes))
    ).reshape(2 * group, c * space)
    own_weight = jnp.broadcast_to(0.5 * jnp.sum(weight_row), (1, mid))
    table = jnp.where(dp == 0, norms[:, 0], 0.0)
    table = jnp.where((jnp.arange(c) == chan)[None, :, None], table[:, None, :], 0.0)
    carried = table.reshape(-1, mid)
    own_weight = jnp.concatenate([own_weight, carried])

    def assembled(parts, shape, wide_rows):
        if parts[0][0].shape[-1] % LANES == 0:
            plan = [masks for _, masks in parts]
            kernel = functools.partial(assemble_kernel, c, plan, wide_rows)
            return call(kernel, [(shape, BF16)], me, *[array for array, _ in parts])[0]
        blocks = jnp.concatenate([array for array, _ in parts], axis=0)
        order = jnp.array([mask for _, masks in parts for mask in masks])
        blocks = jnp.take(blocks, jnp.argsort(order ^ number), axis=0)
        blocks = blocks.reshape((d, c) + blocks.shape[1:])
        return blocks.transpose(1, 2, 0, 3).reshape(shape)

    whole_in = assembled(low_in, (wide, mid), True)
    hidden_one, sums_one = call(
        first_kernel, [((rows, mid), F32), ((2 + own_weight.shape[0], mid), F32)], me, own_weight, *pieces, whole_in,
        flops=2 * rows * wide * mid,
    )
    sums_one, half_way, _ = total(sums_one, n)
    weight_sum = sums_one[2, 0]
    tables = sums_one[3:].reshape(2, c, -1)
    norms_one = tables[:, :, :narrow].reshape(2, mid)
    norms_two = tables[:, :, narrow : 2 * narrow].reshape(2, mid)
    norms_three = tables[:, :, 2 * narrow :].reshape(2, wide)

    low_out, _ = gather_low(high_out, False, n, half_way)
    whole_mid = assembled(low_mid, (9, mid, mid), True).reshape(9 * mid, mid)
    line = size * group
    padded = ((3, rows + 2 * line, mid), jnp.float32)
    cols, hidden_two, sums_two = call(
        functools.partial(second_kernel, count, size, group),
        [((rows, 9 * mid), BF16), ((rows, mid), F32), ((2, mid), F32)],
        me, hidden_one, sums_one, norms_one, whole_mid,
        flops=18 * rows * mid * mid, scratch=[padded],
    )
    whole_head = call(
        functools.partial(assemble_head_kernel, c), [((wide, c * space), BF16)], me, low_head
    )[0]
    sums_two, *_ = total(sums_two, n, None, whole_head)

    whole_out = assembled(low_out, (mid, wide), False)
    act_two, hidden_three, sums_three = call(
        functools.partial(third_kernel, count),
        [((rows, mid), BF16), ((rows, wide), F32), ((2, wide), F32)],
        me, hidden_two, sums_two, norms_two, whole_out,
        flops=2 * rows * mid * wide,
    )
    sums_three, *_ = total(sums_three, n)

    row_weights = jnp.stack([weight_row, weight_row / weight_sum], axis=1)
    upper_three, back_three, packed, _ = call(
        functools.partial(head_kernel, count, pixels, group, classes),
        [((rows, wide), F32), ((3, wide), F32), ((2 * group, wide + c * space), BF16), ((1, 1), F32)],
        me, hidden_three, sums_three, norms_three, row_weights, target, whole_head, *pieces,
        flops=4 * 8 * wide * c * space,
    )
    everything = lax.all_gather(packed, AXES, axis=0, tiled=True)
    back_three, *_ = total(back_three, n)
    loss_sum = back_three[2, 0]

    down_three, upper_two, back_two = call(
        functools.partial(back_three_kernel, count),
        [((rows, wide), BF16), ((rows, mid), F32), ((2, mid), F32)],
        me, upper_three, hidden_three, sums_three, norms_three, back_three, whole_out,
        hidden_two, sums_two, norms_two,
        flops=2 * rows * mid * wide,
    )
    def blocks_of(shape):
        return [((n // 2,) + shape, BF16)] * 2

    masks = slot_masks(n)
    if aligned:
        parts_out = call(
            functools.partial(grad_out_kernel, c, masks), blocks_of(conv_out.shape),
            me, act_two, down_three, flops=2 * rows * mid * wide, scratch=[((mid, wide), BF16)],
        )
    else:
        whole = dot(act_two, down_three, ((0,), (0,))).astype(BF16)
        whole = whole.reshape((c, conv_out.shape[0], d, conv_out.shape[1])).transpose(2, 0, 1, 3)
        whole = whole.reshape((n,) + conv_out.shape)
        parts_out = [jnp.take(whole, jnp.array(row) ^ number, axis=0) for row in masks]
    back_two, half_way, _ = total(back_two, n, None, parts_out[0])
    kept_out, *sends_out = scatter_start(*parts_out, n)
    sends_out = following(sends_out, half_way)

    down_two, upper_one, back_one = call(
        functools.partial(back_two_kernel, count, size, group),
        [((rows, mid), BF16), ((rows, mid), F32), ((2, mid), F32)],
        me, upper_two, hidden_two, sums_two, norms_two, back_two, whole_mid,
        hidden_one, sums_one, norms_one,
        flops=18 * rows * mid * mid, scratch=[padded, ((rows, 9 * mid), BF16)],
    )
    arrived_out = [swap(send, mask, n) for send, mask in zip(sends_out, (2, 4, 6))]
    parts_mid = call(
        functools.partial(grad_mid_kernel, c, masks), blocks_of((9, fan_in, fan_out)),
        me, cols, down_two, flops=18 * rows * mid * mid, scratch=[((9, mid, mid), BF16)],
    )
    kept_mid, *sends_mid = scatter_start(*parts_mid, n)
    back_one, half_way, _ = total(back_one, n, None, sends_mid[2])
    sends_mid = following(sends_mid, half_way)
    far_mid = swap(sends_mid[2], 6, n)
    sums_out = scatter_next(kept_out, arrived_out, n)
    upper_one = following(upper_one, (far_mid, sums_out[0]))
    parts_in = call(
        functools.partial(grad_in_kernel, count, c, masks), blocks_of(conv_in.shape),
        me, upper_one, hidden_one, sums_one, norms_one, back_one, *pieces,
        flops=2 * rows * mid * wide, scratch=[((wide, mid), BF16), ((rows, mid), BF16)],
    )
    last_out = scatter_last(sums_out, n)
    arrived_mid = [swap(sends_mid[0], 2, n), swap(sends_mid[1], 4, n), far_mid]
    kept_in, *sends_in = scatter_start(*parts_in, n)
    arrived_in = [swap(send, mask, n) for send, mask in zip(sends_in, (2, 4, 6))]
    last_mid = scatter_last(scatter_next(kept_mid, arrived_mid, n), n)
    arrived_in, last_mid = lax.optimization_barrier((arrived_in, last_mid))
    sums_in = scatter_next(kept_in, arrived_in, n)
    last_mid = following(last_mid, sums_in[0])
    grad_out = added(last_out)
    grad_mid = added(last_mid).reshape(conv_mid.shape)
    grad_in = added(scatter_last(sums_in, n))

    pooled = lax.dynamic_slice_in_dim(everything, dp * tall, tall, axis=1)
    upper_logits = lax.dynamic_slice_in_dim(everything, wide + chan * space, space, axis=1)
    grad_head = 0.5 * dot(pooled, upper_logits, ((0,), (0,)))[:, :classes]

    def mine(sums, width):
        return lax.dynamic_slice_in_dim(sums[:2], chan * width, width, axis=1)[::-1]

    grad_norms = jnp.concatenate(
        [mine(back_one, narrow), mine(back_two, narrow), mine(back_three, deep)], axis=1
    )[:, None, :]
    params = (conv_in, conv_mid, conv_out, classifier, norms)
    grads = (grad_in, grad_mid, grad_out, grad_head, grad_norms)
    moments = (momentum_in, momentum_mid, momentum_out, momentum_head, momentum_norms)
    averages = (average_in, average_mid, average_out, average_head, average_norms)
    rates = (RATE_MATRIX, RATE_MATRIX, RATE_MATRIX, RATE_MATRIX, RATE_NORM)
    results = [
        advance(p, g, m, a, r) for p, g, m, a, r in zip(params, grads, moments, averages, rates)
    ]
    news = [item[0] for item in results]
    freshs = [item[1] for item in results]
    means = [item[2] for item in results]
    copies = [item.astype(BF16) for item in news]
    return (loss_sum, weight_sum, *news, *freshs, *means, *copies)


def solution(mesh):
    matrices = (P("dp", "chan"), P(None, None, "dp", "chan"), P("chan", "dp"), P("dp", "chan"), P(None, "chan", None))
    return jax.shard_map(
        functools.partial(shards, mesh.shape["dp"], mesh.shape["chan"]),
        mesh=mesh,
        in_specs=(P("dp", None, None, "chan"), P("dp"), P()) + matrices * 3,
        out_specs=(P(), P()) + matrices * 4,
        check_vma=False,
    )
```

```python
import functools
import math

import jax
import jax.numpy as jnp
from jax import lax
from jax.experimental import pallas as pl
from jax.experimental.pallas import tpu as pltpu
from jax.sharding import PartitionSpec as P

EPS = 1e-05
MOMENTUM = 0.5
AVERAGE = 0.5
RATE_MATRIX = 16.0
RATE_NORM = 64.0
AXES = ("dp", "chan")
F32 = jnp.float32
BF16 = jnp.bfloat16
CHUNK = 80
LANES = 128


def swap(array, mask, n):
    return lax.ppermute(array, AXES, [(d, d ^ mask) for d in range(n)])


def tree_sum(parts):
    while len(parts) > 1:
        parts = [parts[k] + parts[k + 1] for k in range(0, len(parts), 2)]
    return parts[0]


def high_masks(n):
    return [8 * k for k in range(n // 8)]


def total(array, n, late=None, paired=False):
    pair = array if paired else array + swap(array, 1, n)
    array = tree_sum([pair] + [swap(pair, mask, n) for mask in (2, 4, 6)])
    array = following(array, late)
    return tree_sum([array] + [swap(array, mask, n) for mask in high_masks(n)[1:]]), array


def following(value, earlier):
    return value if earlier is None else lax.optimization_barrier((value, earlier))[0]


def gather_high(shard, n):
    return [shard] + [swap(shard, mask, n) for mask in high_masks(n)[1:]]


def gather_low(parts, halves, n, after=None):
    stack, masks = following(jnp.stack(parts), after), high_masks(n)
    near, side = swap(stack, 2, n), swap(stack, 4, n)
    half = len(masks) // 2
    pairs = [(stack, masks), (side, [m ^ 4 for m in masks]), (near, [m ^ 2 for m in masks])]
    if halves:
        pairs.append((swap(near[:half], 4, n), [m ^ 6 for m in masks[:half]]))
        pairs.append((swap(side[half:], 2, n), [m ^ 6 for m in masks[half:]]))
    else:
        pairs.append((swap(stack, 6, n), [m ^ 6 for m in masks]))
    pairs += [(swap(array, 1, n), [m ^ 1 for m in row]) for array, row in pairs]
    return pairs, side


def slot_masks(n):
    return [[core ^ low ^ high for low in (0, 2, 4, 6) for high in high_masks(n)] for core in (0, 1)]


def scatter_start(own, other, n):
    outs = [((n // 8,) + own.shape[1:], BF16)] * 4
    return call(add_quarters_kernel, outs, swap(other, 1, n), own, anywhere=True)


def scatter_next(kept, arrived, n):
    shape = kept.shape[1:]
    outs = [(shape, F32)] + [(shape, BF16)] * (n // 8 - 1)
    return call(add_next_kernel, outs, kept, *arrived, anywhere=True)


def split_start(own, other, plan, n):
    shape = own.shape[1:]
    halves = [((n // 4, stop - start) + shape[1:], BF16) for start, stop, _ in plan for _ in (0, 1)]
    outs = call(functools.partial(add_first_kernel, plan), halves, swap(other, 1, n), own, anywhere=True)
    return outs[0::2], outs[1::2]


def split_second(arrived, keeps, n):
    quarters = [((n // 8,) + keep.shape[1:], BF16) for keep in keeps for _ in (0, 1)]
    outs = call(add_second_kernel, quarters, *arrived, *keeps, anywhere=True)
    return outs[0::2], outs[1::2]


def split_third(arrived, keeps, plan, n):
    shape = (plan[-1][1],) + keeps[0].shape[2:]
    outs = [(shape, F32)] + [(shape, BF16)] * (n // 8 - 1)
    return call(functools.partial(add_third_kernel, plan), outs, *arrived, *keeps, anywhere=True)


def scatter_last(sums, n):
    return [sums[0]] + [swap(part, mask, n) for part, mask in zip(sums[1:], high_masks(n)[1:])]


def added(parts):
    return tree_sum([part.astype(F32) for part in parts])


def call(kernel, outs, *inputs, flops=0, anywhere=False, scratch=(), semaphores=(), remain=0):
    first = len(inputs) - remain
    inputs = [pltpu.with_memory_space_constraint(x, pltpu.HBM) if k >= first else x for k, x in enumerate(inputs)]
    moved = sum(x.size * x.dtype.itemsize for x in inputs)
    shapes = [jax.ShapeDtypeStruct(*out) for out in outs]
    moved += sum(s.size * s.dtype.itemsize for s in shapes)
    held = sum(math.prod(shape) * dtype(0).itemsize for shape, dtype in scratch)
    specs = [pl.BlockSpec(memory_space=pltpu.VMEM if k < first else pltpu.HBM) for k in range(len(inputs))]
    if not anywhere:
        specs[0] = pl.BlockSpec(memory_space=pltpu.SMEM)
    return pl.pallas_call(
        kernel,
        out_shape=shapes,
        in_specs=specs,
        out_specs=[pl.BlockSpec(memory_space=pltpu.VMEM)] * len(outs),
        scratch_shapes=[pltpu.VMEM(*one) for one in scratch] + list(semaphores),
        compiler_params=pltpu.CompilerParams(vmem_limit_bytes=max(moved // 2, 8 * 2**20) + held + 4 * 2**20),
        cost_estimate=pl.CostEstimate(flops=flops, bytes_accessed=moved, transcendentals=0),
    )(*inputs)


def sigmoid(value):
    return 0.5 * jnp.tanh(0.5 * value) + 0.5


def silu_grad(value):
    sigma = sigmoid(value)
    return sigma * (1.0 + value * (1.0 - sigma))


def dot(a, b, dims=((1,), (0,))):
    return lax.dot_general(a, b, (dims, ((), ())), preferred_element_type=F32)


def statistics(sums_ref, count, cols):
    mean = sums_ref[0:1, cols] / count
    square = sums_ref[1:2, cols] / count
    return mean, lax.rsqrt(square - mean * mean + EPS)


def col_sum(value):
    return jnp.sum(value, axis=0, keepdims=True)


def octet_sum(value):
    return jnp.sum(value.reshape(value.shape[0] // 8, 8, value.shape[1]), axis=0)


def rows_of(step):
    return pl.ds(pl.multiple_of(step * CHUNK, CHUNK), CHUNK)


def at(index, size):
    if isinstance(index, int):
        return pl.ds(index * size, size)
    return pl.ds(pl.multiple_of(index * size, size), size)


def assemble_kernel(c, plan, me, *refs):
    *parts, out = refs
    number = me[0] * c + me[1]
    for part, masks in zip(parts, plan):
        for a, mask in enumerate(masks):
            other = number ^ mask
            i, j = lax.div(other, c), lax.rem(other, c)
            rows, cols = part.shape[1:]
            out[at(i, rows), at(j, cols)] = part[a]


def assemble_mid_kernel(c, plan, me, *refs):
    parts, outs = refs[: len(plan)], refs[len(plan) :]
    number = me[0] * c + me[1]
    for part, masks in zip(parts, plan):
        for a, mask in enumerate(masks):
            other = number ^ mask
            i, j = lax.div(other, c), lax.rem(other, c)
            rows, cols = part.shape[2:]
            outs[0][:, at(i, rows), at(j, cols)] = part[a, 0:9]
            if len(outs) > 1:
                for k in range(4):
                    outs[1][at(2 * j + k // 2, rows), at(2 * i + k % 2, cols)] = part[a, 9 + k]


def prepare_kernel(c, me, *refs):
    sources, outs, held, arrived = refs[:5], refs[5:-6], refs[-6:-1], refs[-1]
    pieces, (low_in, low_mid, low_head) = outs[:c], outs[c:]
    features, conv_in, conv_mid, conv_out, classifier = held
    order = (1, 0, 2, 3, 4)
    copies = [pltpu.make_async_copy(sources[k], held[k], arrived.at[k]) for k in range(5)]
    for k in order:
        copies[k].start()
    copies[1].wait()
    low_in[...] = conv_in[...].astype(BF16)
    copies[0].wait()
    pixels, images, width = features.shape
    group = images // c
    for t in range(c):
        part = features[:, t * group : (t + 1) * group, :].astype(F32)
        part = part.reshape(pixels * group, width).astype(BF16)
        for k in range(c):

            @pl.when(me[1] == t ^ k)
            def _(part=part, k=k):
                pieces[k][...] = part

    copies[2].wait()
    low_mid[0:9] = conv_mid[...].astype(BF16)
    copies[3].wait()
    if low_mid.shape[0] > 9:
        rows, cols = low_mid.shape[1:]
        for k in range(4):
            part = conv_out[k // 2 * rows : (k // 2 + 1) * rows, k % 2 * cols : (k % 2 + 1) * cols]
            low_mid[9 + k] = part.astype(BF16)
    copies[4].wait()
    tall, classes = classifier.shape
    for k, start in enumerate(range(0, classes, LANES)):
        stop = min(start + LANES, classes)
        rows = slice(k * tall, (k + 1) * tall)
        low_head[rows, 0 : stop - start] = classifier[:, start:stop].astype(BF16)
        if stop - start < LANES:
            low_head[rows, stop - start :] = jnp.zeros((tall, LANES - stop + start), BF16)


def fetch(sources, places, arrived, start=0):
    copies = [pltpu.make_async_copy(x, y, arrived.at[start + k]) for k, (x, y) in enumerate(zip(sources, places))]
    for copy in copies:
        copy.start()
    return copies


def first_kernel(c, me, carried, weights, *refs):
    features, (hidden, sums, held, arrived) = refs[:c], refs[c:]
    chan, depth = me[1], features[0].shape[1]
    width = hidden.shape[1]
    copies = fetch(features, [held.at[k] for k in range(c)], arrived)
    for start in range(0, width, 256):
        cols = slice(start, start + 256)
        value = None
        for k in range(c):
            if start == 0:
                copies[k].wait()
            rows = pl.ds(pl.multiple_of((chan ^ k) * depth, depth), depth)
            term = dot(held[k], weights[rows, cols])
            value = term if value is None else value + term
        hidden[:, cols] = value
        sums[0:1, cols] = col_sum(value)
        sums[1:2, cols] = col_sum(value * value)
    sums[2:, :] = carried[...]


def windows(pad, out, size, group):
    line = size * group
    rows, width = out.shape[0], pad.shape[2]
    for i in range(3):
        for j in range(3):
            tap = 3 * i + j
            out[:, tap * width : (tap + 1) * width] = pad[
                j, i * line : i * line + rows, :
            ].astype(BF16)


def fill(pad, size, group):
    line = size * group
    rows, width = pad.shape[1] - 2 * line, pad.shape[2]
    place = lax.broadcasted_iota(jnp.int32, (rows, 1), 0)
    column = lax.rem(lax.div(place, group), size)
    here = pad[1, line : line + rows, :]
    empty = jnp.zeros((line, width), F32)
    for j in (0, 2):
        moved = pltpu.roll(here, group if j == 0 else rows - group, 0)
        valid = column != (0 if j == 0 else size - 1)
        pad[j, 0:line, :] = empty
        pad[j, line : line + rows, :] = jnp.where(valid, moved, 0.0)
        pad[j, line + rows :, :] = empty


def second_kernel(count, size, group, me, hidden, sums, norms, weights, low_act, out, out_sums, pad, cols):
    rows, width = hidden.shape
    line = size * group
    mean, scale = statistics(sums, count, slice(None))
    gain, shift = norms[0:1, :], norms[1:2, :]
    pad[1, 0:line, :] = jnp.zeros((line, width), F32)
    pad[1, line + rows :, :] = jnp.zeros((line, width), F32)
    for step in range(rows // CHUNK):
        part = slice(step * CHUNK, (step + 1) * CHUNK)
        value = (hidden[part, :] - mean) * scale * gain + shift
        act = (value * sigmoid(value)).astype(BF16)
        low_act[part, :] = act
        pad[1, line + step * CHUNK : line + (step + 1) * CHUNK, :] = act.astype(F32)
    fill(pad, size, group)
    windows(pad, cols, size, group)
    for start in range(0, out.shape[1], 256):
        block = slice(start, start + 256)
        value = dot(cols[...], weights[:, block])
        out[:, block] = value
        out_sums[0:1, block] = col_sum(value)
        out_sums[1:2, block] = col_sum(value * value)


def third_kernel(count, me, hidden, sums, norms, weights, act, out, out_sums):
    mean, scale = statistics(sums, count, slice(None))
    gain, shift = norms[0:1, :], norms[1:2, :]
    for step in range(hidden.shape[0] // CHUNK):
        part = slice(step * CHUNK, (step + 1) * CHUNK)
        value = (hidden[part, :] - mean) * scale * gain + shift
        act[part, :] = (value * sigmoid(value)).astype(BF16)
    for start in range(0, out.shape[1], 256):
        block = slice(start, start + 256)
        value = dot(act[...], weights[:, block])
        out[:, block] = value
        out_sums[0:1, block] = col_sum(value)
        out_sums[1:2, block] = col_sum(value * value)


def head_kernel(count, pixels, group, classes, c, me, hidden, sums, norms, row_weights, target, shards, *refs):
    sources, (upper, out_sums, packed, loss, features, weights, arrived) = refs[:c], refs[c:]
    chan, rows = me[1], hidden.shape[0]
    width = features.shape[2]
    twice = 2 * group
    copies = fetch(sources, [features.at[k] for k in range(c)], arrived)
    devices, tall = shards.shape[0], weights.shape[0] * c // shards.shape[0]
    halves = weights.shape[1] // (c * LANES)
    copies += fetch(
        [shards.at[a, pl.ds(k * tall, tall), :] for a in range(devices) for k in range(halves)],
        [
            weights.at[pl.ds(a // c * tall, tall), pl.ds((a % c * halves + k) * LANES, LANES)]
            for a in range(devices)
            for k in range(halves)
        ],
        arrived,
        c,
    )
    blocks = [pl.ds(pl.multiple_of((chan ^ k) * width, width), width) for k in range(c)]
    for k, cols in enumerate(blocks):
        mean, scale = statistics(sums, count, cols)
        gain = scale * norms[0:1, cols]
        shift = norms[1:2, cols] - mean * gain
        copies[k].wait()

        def forward(step, pool, k=k, cols=cols, gain=gain, shift=shift):
            part = rows_of(step)
            value = hidden[part, cols] * gain + shift + features[k, part, :].astype(F32)
            sigma = sigmoid(value)
            value = value * sigma
            upper[part, cols] = sigma + value - value * sigma
            return pool + jnp.sum(value.reshape(CHUNK // twice, twice, width), axis=0)

        pool = lax.fori_loop(0, rows // CHUNK, forward, jnp.zeros((twice, width), F32))
        pool = (pool + pltpu.roll(pool, group, 0)) / pixels
        packed[:, cols] = pool.astype(BF16)
    depth, space = weights.shape
    for copy in copies[c:]:
        copy.wait()
    pooled = packed[:, 0:depth]
    logits = dot(pooled, weights[...])
    column = lax.broadcasted_iota(jnp.int32, logits.shape, 1)
    valid = lax.rem(column, space // c) < classes
    top = jnp.max(jnp.where(valid, logits, -jnp.inf), axis=1, keepdims=True)
    grown = jnp.where(valid, jnp.exp(logits - top), 0.0)
    spread = top + jnp.log(jnp.sum(grown, axis=1, keepdims=True))
    wanted = target[...]
    picked = jnp.sum(wanted * logits, axis=1, keepdims=True)
    weight, share = row_weights[:, 0:1], row_weights[:, 1:2]
    loss[...] = 0.5 * jnp.sum(weight * (spread - picked), axis=0, keepdims=True)
    down = share * (jnp.where(valid, jnp.exp(logits - spread), 0.0) - wanted)
    packed[:, depth:] = down.astype(BF16)
    low_down = down.astype(BF16)
    for k, cols in enumerate(blocks):
        mean, scale = statistics(sums, count, cols)
        back = dot(low_down, weights[cols, :], ((1,), (1,))) / pixels
        back = jnp.broadcast_to(back[None], (CHUNK // twice, twice, width)).reshape(CHUNK, width)

        def backward(step, so_far, cols=cols, mean=mean, back=back):
            part = rows_of(step)
            value = back * upper[part, cols]
            moved = value * (hidden[part, cols] - mean)
            upper[part, cols] = value
            return (so_far[0] + octet_sum(value), so_far[1] + octet_sum(moved))

        zero = jnp.zeros((8, width), F32)
        first, second = lax.fori_loop(0, rows // CHUNK, backward, (zero, zero))
        out_sums[0:1, cols] = col_sum(first)
        out_sums[1:2, cols] = col_sum(second) * scale
    wide = hidden.shape[1]
    out_sums[:, wide:] = jnp.broadcast_to(loss[...], (2, out_sums.shape[1] - wide))


def lower(upper, hidden, sums, back_sums, norms, count, part, cols):
    mean, scale = statistics(sums, count, cols)
    normed = (hidden[part, cols] - mean) * scale
    slope = scale * norms[0:1, cols]
    return slope * (
        upper[part, cols] - back_sums[0:1, cols] / count - normed * (back_sums[1:2, cols] / count)
    )


def back_three_kernel(
    count, me, upper, hidden, sums, norms, back_sums, weights, hidden_two, sums_two, norms_two, down, out, out_sums
):
    rows, wide = upper.shape
    for start in range(0, wide, 512):
        cols = slice(start, start + 512)
        for step in range(rows // CHUNK):
            part = slice(step * CHUNK, (step + 1) * CHUNK)
            down[part, cols] = lower(
                upper, hidden, sums, back_sums, norms, count, part, cols
            ).astype(BF16)
    for start in range(0, out.shape[1], 256):
        cols = slice(start, start + 256)
        value = dot(down[...], weights[cols, :], ((1,), (1,)))
        finish(value, hidden_two, sums_two, norms_two, count, cols, out, out_sums)


def finish(value, hidden, sums, norms, count, cols, out, out_sums):
    mean, scale = statistics(sums, count, cols)
    normed = (hidden[:, cols] - mean) * scale
    value = value * silu_grad(normed * norms[0:1, cols] + norms[1:2, cols])
    out[:, cols] = value
    out_sums[0:1, cols] = col_sum(value)
    out_sums[1:2, cols] = col_sum(value * normed)


def back_two_kernel(
    count, size, group, me, upper, hidden, sums, norms, back_sums, weights, hidden_one, sums_one, norms_one,
    down, out, out_sums, pad, cols,
):
    rows, width = upper.shape
    line = size * group
    pad[1, 0:line, :] = jnp.zeros((line, width), F32)
    pad[1, line + rows :, :] = jnp.zeros((line, width), F32)
    for step in range(rows // CHUNK):
        part = slice(step * CHUNK, (step + 1) * CHUNK)
        value = lower(upper, hidden, sums, back_sums, norms, count, part, slice(None)).astype(BF16)
        down[part, :] = value
        pad[1, line + step * CHUNK : line + (step + 1) * CHUNK, :] = value.astype(F32)
    fill(pad, size, group)
    windows(pad, cols, size, group)
    for start in range(0, out.shape[1], 256):
        block = slice(start, start + 256)
        value = None
        for tap in range(9):
            base = (8 - tap) * out.shape[1] + start
            term = dot(
                cols[:, tap * width : (tap + 1) * width],
                weights[base : base + 256, :],
                ((1,), (1,)),
            )
            value = term if value is None else value + term
        finish(value, hidden_one, sums_one, norms_one, count, block, out, out_sums)


def spread_blocks(number, c, outs, masks, block):
    for out, row in zip(outs, masks):
        for a, mask in enumerate(row):
            other = number ^ mask
            out[a] = block(lax.div(other, c), lax.rem(other, c))


def turned(value):
    return value.astype(F32).T.astype(BF16)


def grad_mid_kernel(c, masks, size, group, me, act, down, act_two, down_three, *refs):
    *outs, whole, pad, cols, whole_out = refs
    rows, depth = act.shape
    line = size * group
    pad[1, 0:line, :] = jnp.zeros((line, depth), F32)
    pad[1, line + rows :, :] = jnp.zeros((line, depth), F32)
    pad[1, line : line + rows, :] = down[...].astype(F32)
    fill(pad, size, group)
    windows(pad, cols, size, group)
    left = turned(act[...])
    for tap in range(9):
        whole[tap] = dot(left, cols[:, (8 - tap) * depth : (9 - tap) * depth]).astype(BF16)
    left = turned(act_two[...])
    wide = whole_out.shape[1]
    for start in range(0, wide, 512):
        part = slice(start, start + 512)
        whole_out[:, part] = dot(left, down_three[:, part]).astype(BF16)
    height, width = outs[0].shape[2:]
    number = me[0] * c + me[1]
    for out, row in zip(outs, masks):
        for a, mask in enumerate(row):
            other = number ^ mask
            i, j = lax.div(other, c), lax.rem(other, c)
            out[a, 0:9] = whole[:, at(i, height), at(j, width)]
            for k in range(4):
                out[a, 9 + k] = whole_out[at(2 * j + k // 2, height), at(2 * i + k % 2, width)]


def grad_in_kernel(count, c, masks, me, upper, hidden, sums, norms, back_sums, *refs):
    sources, outs, (whole, down, features, arrived) = refs[:c], refs[c:-4], refs[-4:]
    copies = fetch(sources, [features.at[k] for k in range(c)], arrived)
    rows = upper.shape[0]
    for step in range(rows // CHUNK):
        part = slice(step * CHUNK, (step + 1) * CHUNK)
        down[part, :] = lower(
            upper, hidden, sums, back_sums, norms, count, part, slice(None)
        ).astype(BF16)
    depth = features.shape[2]
    for k in range(c):
        copies[k].wait()
        whole[at(me[1] ^ k, depth), :] = dot(features[k], down[...], ((0,), (0,))).astype(BF16)
    height, width = outs[0].shape[1:]
    spread_blocks(
        me[0] * c + me[1], c, outs, masks, lambda i, j: whole[at(i, height), at(j, width)]
    )


def add_low(one, other):
    return (one.astype(F32) + other.astype(F32)).astype(BF16)


def add_quarters_kernel(arrived, own, *outs):
    z = own.shape[0] // 4
    for low, out in enumerate(outs):
        for k in range(z):
            out[k] = add_low(own[low * z + k], arrived[low * z + k])


def add_first_kernel(plan, arrived, own, *outs):
    z = own.shape[0] // 4
    for (start, stop, order), send, keep in zip(plan, outs[0::2], outs[1::2]):
        for low in range(4):
            inside = low // 2 if order[0] == 2 else low % 2
            out = send if low & (order[0] // 2) else keep
            for k in range(z):
                entry = low * z + k
                out[inside * z + k] = add_low(own[entry, start:stop], arrived[entry, start:stop])


def add_second_kernel(*refs):
    parts = len(refs) // 4
    arrived, keeps, outs = refs[:parts], refs[parts : 2 * parts], refs[2 * parts :]
    for one, other, send, keep in zip(arrived, keeps, outs[0::2], outs[1::2]):
        z = send.shape[0]
        for k in range(z):
            keep[k] = add_low(one[k], other[k])
            send[k] = add_low(one[z + k], other[z + k])


def add_third_kernel(plan, *refs):
    parts = len(plan)
    arrived, keeps, outs = refs[:parts], refs[parts : 2 * parts], refs[2 * parts :]
    for (start, stop, _), one, other in zip(plan, arrived, keeps):
        for k, out in enumerate(outs):
            value = one[k].astype(F32) + other[k].astype(F32)
            out[start:stop] = value if k == 0 else value.astype(BF16)


def add_next_kernel(kept, one, two, three, *outs):
    for k, out in enumerate(outs):
        pair = kept[k].astype(F32) + one[k].astype(F32)
        out[...] = (pair + (two[k].astype(F32) + three[k].astype(F32))).astype(out.dtype)


def advance(weight, grad, momentum, average, rate):
    fresh = MOMENTUM * momentum + grad
    weight_new = weight - rate * (grad + MOMENTUM * fresh)
    return (weight_new, fresh, AVERAGE * average + (1.0 - AVERAGE) * weight_new)


def shards(
    d,
    c,
    features,
    labels,
    class_weights,
    conv_in,
    conv_mid,
    conv_out,
    classifier,
    norms,
    momentum_in,
    momentum_mid,
    momentum_out,
    momentum_head,
    momentum_norms,
    average_in,
    average_mid,
    average_out,
    average_head,
    average_norms,
):
    n = d * c
    dp, chan = lax.axis_index("dp"), lax.axis_index("chan")
    number = dp * c + chan
    me = jnp.stack([dp, chan]).astype(jnp.int32)
    images, size = features.shape[0], features.shape[1]
    group = images // c
    pixels = size * size
    count = float(images * pixels * d)
    rows = pixels * group
    deep = features.shape[3]
    mid, wide = conv_in.shape[1] * c, deep * c
    aligned = conv_out.shape[1] % LANES == 0

    fan_in, fan_out = conv_mid.shape[2:]
    classes = classifier.shape[1]
    space = -(-classes // LANES) * LANES
    tall = classifier.shape[0]
    laid = features.transpose(1, 2, 0, 3).reshape(pixels, images, deep)
    narrow_mid = conv_mid.reshape(9, fan_in, fan_out)
    sources = (laid, conv_in, narrow_mid, conv_out, classifier)
    own, mate, other, away, low_in, low_mid, low_head = call(
        functools.partial(prepare_kernel, c),
        [((rows, deep), BF16)] * c
        + [(conv_in.shape, BF16), ((13 if aligned else 9, fan_in, fan_out), BF16)]
        + [((tall * (space // LANES), LANES), BF16)],
        me, *sources, remain=5,
        scratch=[(x.shape, jnp.dtype(x.dtype).type) for x in sources],
        semaphores=[pltpu.SemaphoreType.DMA((5,))],
    )
    if not aligned:
        low_mid = jnp.concatenate([low_mid, conv_out.astype(BF16).reshape(4, fan_in, fan_out)])
    away, other = swap(away, 2, n), swap(other, 2, n)
    high_in = gather_high(low_in, n)
    low_head = lax.all_gather(low_head, AXES)
    pieces = [own, swap(mate, 1, n), other, swap(away, 1, n)]
    low_in, side_in = gather_low(high_in, False, n, (away, other))
    high_mid = gather_high(following(low_mid, high_in[1]), n)
    low_mid, _ = gather_low(high_mid, True, n, side_in)

    narrow = conv_in.shape[1]
    own = lax.dynamic_index_in_dim(labels.reshape(c, group), chan, 0, keepdims=False)
    own = jnp.concatenate([own, own])
    catalog = lax.broadcasted_iota(jnp.int32, (2 * group, class_weights.shape[0]), 1)
    chosen = catalog == own[:, None]
    weight_row = jnp.sum(jnp.where(chosen, class_weights[None, :], 0), axis=1).astype(F32)
    target = jnp.pad(
        chosen.astype(F32).reshape(2 * group, c, classes), ((0, 0), (0, 0), (0, space - classes))
    ).reshape(2 * group, c * space)
    own_weight = jnp.broadcast_to(0.5 * jnp.sum(weight_row), (1, mid))
    table = jnp.where(dp == 0, norms[:, 0], 0.0)
    table = jnp.where((jnp.arange(c) == chan)[None, :, None], table[:, None, :], 0.0)
    carried = table.reshape(-1, mid)
    own_weight = jnp.concatenate([own_weight, carried])

    def assembled(kernel, parts, *shapes):
        kernel = functools.partial(kernel, c, [masks for _, masks in parts])
        return call(kernel, [(shape, BF16) for shape in shapes], me, *[array for array, _ in parts])

    (whole_in,) = assembled(assemble_kernel, low_in, (wide, mid))
    feature_space = [((c, rows, deep), jnp.bfloat16)]
    feature_ends = [pltpu.SemaphoreType.DMA((c,))]
    hidden_one, sums_one = call(
        functools.partial(first_kernel, c),
        [((rows, mid), F32), ((2 + own_weight.shape[0], mid), F32)], me, own_weight, whole_in, *pieces,
        flops=2 * rows * wide * mid, scratch=feature_space, semaphores=feature_ends, remain=c,
    )
    sums_one, *_ = total(sums_one, n)
    weight_sum = sums_one[2, 0]
    tables = sums_one[3:].reshape(2, c, -1)
    norms_one = tables[:, :, :narrow].reshape(2, mid)
    norms_two = tables[:, :, narrow : 2 * narrow].reshape(2, mid)
    norms_three = tables[:, :, 2 * narrow :].reshape(2, wide)

    if aligned:
        whole_mid, whole_out = assembled(assemble_mid_kernel, low_mid, (9, mid, mid), (mid, wide))
    else:
        (whole_mid,) = assembled(assemble_mid_kernel, low_mid, (9, mid, mid))
        blocks = jnp.concatenate([array[:, 9:] for array, _ in low_mid])
        order = jnp.array([mask for _, masks in low_mid for mask in masks])
        blocks = jnp.take(blocks, jnp.argsort(order ^ number), axis=0)
        blocks = blocks.reshape((d, c) + conv_out.shape)
        whole_out = blocks.transpose(1, 2, 0, 3).reshape(mid, wide)
    whole_mid = whole_mid.reshape(9 * mid, mid)
    line = size * group
    padded = ((3, rows + 2 * line, mid), jnp.float32)
    many = ((rows, 9 * mid), jnp.bfloat16)
    act_one, hidden_two, sums_two = call(
        functools.partial(second_kernel, count, size, group),
        [((rows, mid), BF16), ((rows, mid), F32), ((2, mid), F32)],
        me, hidden_one, sums_one, norms_one, whole_mid,
        flops=18 * rows * mid * mid, scratch=[padded, many],
    )
    sums_two, *_ = total(sums_two, n)

    act_two, hidden_three, sums_three = call(
        functools.partial(third_kernel, count),
        [((rows, mid), BF16), ((rows, wide), F32), ((2, wide), F32)],
        me, hidden_two, sums_two, norms_two, whole_out,
        flops=2 * rows * mid * wide,
    )
    sums_three, *_ = total(sums_three, n)

    row_weights = jnp.stack([weight_row, weight_row / weight_sum], axis=1)
    upper_three, back_three, packed, _ = call(
        functools.partial(head_kernel, count, pixels, group, classes, c),
        [((rows, wide), F32), ((2, wide + LANES), F32), ((2 * group, wide + c * space), BF16), ((1, 1), F32)],
        me, hidden_three, sums_three, norms_three, row_weights, target, low_head, *pieces,
        flops=4 * 8 * wide * c * space, remain=1 + c,
        scratch=feature_space + [((wide, c * space), jnp.bfloat16)],
        semaphores=[pltpu.SemaphoreType.DMA((c + n * (space // LANES),))],
    )
    everything = lax.all_gather(packed, AXES, axis=0, tiled=True)
    back_three, *_ = total(back_three, n)
    loss_sum = back_three[0, wide]

    down_three, upper_two, back_two = call(
        functools.partial(back_three_kernel, count),
        [((rows, wide), BF16), ((rows, mid), F32), ((2, mid), F32)],
        me, upper_three, hidden_three, sums_three, norms_three, back_three, whole_out,
        hidden_two, sums_two, norms_two,
        flops=2 * rows * mid * wide,
    )
    def blocks_of(shape):
        return [((n // 2,) + shape, BF16)] * 2

    masks = slot_masks(n)
    back_two, *_ = total(back_two, n)

    down_two, upper_one, back_one = call(
        functools.partial(back_two_kernel, count, size, group),
        [((rows, mid), BF16), ((rows, mid), F32), ((2, mid), F32)],
        me, upper_two, hidden_two, sums_two, norms_two, back_two, whole_mid,
        hidden_one, sums_one, norms_one,
        flops=18 * rows * mid * mid, scratch=[padded, many],
    )

    back_one = back_one + swap(back_one, 1, n)
    down_two = following(down_two, back_one)
    if aligned:
        parts_mid = call(
            functools.partial(grad_mid_kernel, c, masks, size, group), blocks_of((13, fan_in, fan_out)),
            me, act_one, down_two, act_two, down_three, flops=18 * rows * mid * mid,
            scratch=[((9, mid, mid), jnp.bfloat16), padded, many, ((mid, wide), jnp.bfloat16)],
        )
    else:
        pad = jnp.pad(act_one.reshape(size, size, group, mid), ((1, 1), (1, 1), (0, 0), (0, 0)))
        whole = [
            dot(pad[i : i + size, j : j + size].reshape(rows, mid), down_two, ((0,), (0,))).astype(BF16)
            for i in range(3)
            for j in range(3)
        ]
        whole = jnp.stack(whole).reshape(9, d, fan_in, c, fan_out).transpose(1, 3, 0, 2, 4)
        whole_two = dot(act_two, down_three, ((0,), (0,))).astype(BF16)
        whole_two = whole_two.reshape((c, conv_out.shape[0], d, conv_out.shape[1])).transpose(2, 0, 1, 3)
        whole_two = whole_two.reshape(d, c, 4, fan_in, fan_out)
        whole = jnp.concatenate([whole, whole_two], axis=2).reshape(n, 13, fan_in, fan_out)
        parts_mid = [jnp.take(whole, jnp.array(row) ^ number, axis=0) for row in masks]
    plan = [(0, 7, (4, 2)), (7, 13, (2, 4))]
    sends, keeps = split_start(*parts_mid, plan, n)
    back_one, half_way = total(back_one, n, sends[0], True)
    sends = following(sends, half_way)
    arrived = [swap(send, order[0], n) for send, (_, _, order) in zip(sends, plan)]
    sends, keeps = split_second(arrived, keeps, n)
    upper_one = following(upper_one, sends)
    parts_in = call(
        functools.partial(grad_in_kernel, count, c, masks), blocks_of(conv_in.shape),
        me, upper_one, hidden_one, sums_one, norms_one, back_one, *pieces,
        flops=2 * rows * mid * wide, remain=c, semaphores=feature_ends,
        scratch=[((wide, mid), jnp.bfloat16), ((rows, mid), jnp.bfloat16)] + feature_space,
    )
    arrived = [swap(send, order[1], n) for send, (_, _, order) in zip(sends, plan)]
    kept_in, *sends_in = scatter_start(*parts_in, n)
    last_mid = scatter_last(split_third(arrived, keeps, plan, n), n)
    arrived_in = [swap(send, mask, n) for send, mask in zip(sends_in, (2, 4, 6))]
    arrived_in, last_mid = lax.optimization_barrier((arrived_in, last_mid))
    sums_in = scatter_next(kept_in, arrived_in, n)
    last_mid = following(last_mid, sums_in[0])
    grad_mid = added(last_mid)
    grad_mid, grad_out = grad_mid[:9].reshape(conv_mid.shape), grad_mid[9:]
    if aligned:
        grad_out = grad_out.reshape(2, 2, fan_in, fan_out).transpose(0, 2, 1, 3)
    grad_out = grad_out.reshape(conv_out.shape)
    grad_in = added(scatter_last(sums_in, n))

    everything = following(everything, sums_in[0])
    pooled = lax.dynamic_slice_in_dim(everything, dp * tall, tall, axis=1)
    upper_logits = lax.dynamic_slice_in_dim(everything, wide + chan * space, space, axis=1)
    grad_head = 0.5 * dot(pooled, upper_logits, ((0,), (0,)))[:, :classes]

    def mine(sums, width):
        return lax.dynamic_slice_in_dim(sums[:2], chan * width, width, axis=1)[::-1]

    grad_norms = jnp.concatenate(
        [mine(back_one, narrow), mine(back_two, narrow), mine(back_three, deep)], axis=1
    )[:, None, :]
    params = (conv_in, conv_mid, conv_out, classifier, norms)
    grads = (grad_in, grad_mid, grad_out, grad_head, grad_norms)
    moments = (momentum_in, momentum_mid, momentum_out, momentum_head, momentum_norms)
    averages = (average_in, average_mid, average_out, average_head, average_norms)
    rates = (RATE_MATRIX, RATE_MATRIX, RATE_MATRIX, RATE_MATRIX, RATE_NORM)
    results = [
        advance(p, g, m, a, r) for p, g, m, a, r in zip(params, grads, moments, averages, rates)
    ]
    news = [item[0] for item in results]
    freshs = [item[1] for item in results]
    means = [item[2] for item in results]
    copies = [item.astype(BF16) for item in news]
    return (loss_sum, weight_sum, *news, *freshs, *means, *copies)


def solution(mesh):
    matrices = (P("dp", "chan"), P(None, None, "dp", "chan"), P("chan", "dp"), P("dp", "chan"), P(None, "chan", None))
    return jax.shard_map(
        functools.partial(shards, mesh.shape["dp"], mesh.shape["chan"]),
        mesh=mesh,
        in_specs=(P("dp", None, None, "chan"), P("dp"), P()) + matrices * 3,
        out_specs=(P(), P()) + matrices * 4,
        check_vma=False,
    )
```

```python
import functools
import math

import jax
import jax.numpy as jnp
from jax import lax
from jax.experimental import pallas as pl
from jax.experimental.pallas import tpu as pltpu
from jax.sharding import PartitionSpec as P

EPS = 1e-05
MOMENTUM = 0.5
AVERAGE = 0.5
RATE_MATRIX = 16.0
RATE_NORM = 64.0
AXES = ("dp", "chan")
F32 = jnp.float32
BF16 = jnp.bfloat16
CHUNK = 80
LANES = 128


def swap(array, mask, n):
    return lax.ppermute(array, AXES, [(d, d ^ mask) for d in range(n)])


def tree_sum(parts):
    while len(parts) > 1:
        parts = [parts[k] + parts[k + 1] for k in range(0, len(parts), 2)]
    return parts[0]


def high_masks(n):
    return [8 * k for k in range(n // 8)]


def total(array, n, late=None, paired=False):
    pair = array if paired else array + swap(array, 1, n)
    array = tree_sum([pair] + [swap(pair, mask, n) for mask in (2, 4, 6)])
    array = following(array, late)
    return tree_sum([array] + [swap(array, mask, n) for mask in high_masks(n)[1:]]), array


def following(value, earlier):
    return value if earlier is None else lax.optimization_barrier((value, earlier))[0]


def gather_high(shard, n):
    return [shard] + [swap(shard, mask, n) for mask in high_masks(n)[1:]]


def gather_low(parts, halves, n, after=None):
    stack = following(jnp.stack(parts), after)
    near, side = swap(stack, 2, n), swap(stack, 4, n)
    if halves:
        return gather_cross(stack, near, side, n), side
    masks = high_masks(n)
    pairs = list(zip((stack, side, near, swap(stack, 6, n)), ([m ^ low for m in masks] for low in (0, 4, 2, 6))))
    return pairs + [(swap(array, 1, n), [m ^ 1 for m in row]) for array, row in pairs], side


def gather_cross(stack, near, side, n, after=None):
    masks = high_masks(n)
    half = len(masks) // 2
    first, second = following((near[:half], side[half:]), after)
    pairs = [(stack, masks), (side, [m ^ 4 for m in masks]), (near, [m ^ 2 for m in masks])]
    pairs.append((swap(first, 4, n), [m ^ 6 for m in masks[:half]]))
    pairs.append((swap(second, 2, n), [m ^ 6 for m in masks[half:]]))
    return pairs + [(swap(array, 1, n), [m ^ 1 for m in row]) for array, row in pairs]


def slot_masks(n):
    return [[core ^ low ^ high for low in (0, 2, 4, 6) for high in high_masks(n)] for core in (0, 1)]


def scatter_start(own, other, n):
    outs = [((n // 8,) + own.shape[1:], BF16)] * 4
    return call(add_quarters_kernel, outs, swap(other, 1, n), own, anywhere=True)


def scatter_next(kept, arrived, n):
    shape = kept.shape[1:]
    outs = [(shape, F32)] + [(shape, BF16)] * (n // 8 - 1)
    return call(add_next_kernel, outs, kept, *arrived, anywhere=True)


def split_start(own, other, plan, n):
    shape = own.shape[1:]
    halves = [((n // 4, stop - start) + shape[1:], BF16) for start, stop, _ in plan for _ in (0, 1)]
    outs = call(functools.partial(add_first_kernel, plan), halves, swap(other, 1, n), own, anywhere=True)
    return outs[0::2], outs[1::2]


def split_second(arrived, keeps, n):
    quarters = [((n // 8,) + keep.shape[1:], BF16) for keep in keeps for _ in (0, 1)]
    outs = call(add_second_kernel, quarters, *arrived, *keeps, anywhere=True)
    return outs[0::2], outs[1::2]


def split_third(arrived, keeps, plan, n):
    shape = (plan[-1][1],) + keeps[0].shape[2:]
    outs = [(shape, F32)] + [(shape, BF16)] * (n // 8 - 1)
    return call(functools.partial(add_third_kernel, plan), outs, *arrived, *keeps, anywhere=True)


def scatter_last(sums, n):
    return [sums[0]] + [swap(part, mask, n) for part, mask in zip(sums[1:], high_masks(n)[1:])]


def added(parts):
    return tree_sum([part.astype(F32) for part in parts])


def call(kernel, outs, *inputs, flops=0, anywhere=False, scratch=(), semaphores=(), remain=0):
    first = len(inputs) - remain
    inputs = [pltpu.with_memory_space_constraint(x, pltpu.HBM) if k >= first else x for k, x in enumerate(inputs)]
    moved = sum(x.size * x.dtype.itemsize for x in inputs)
    shapes = [jax.ShapeDtypeStruct(*out) for out in outs]
    moved += sum(s.size * s.dtype.itemsize for s in shapes)
    held = sum(math.prod(shape) * dtype(0).itemsize for shape, dtype in scratch)
    specs = [pl.BlockSpec(memory_space=pltpu.VMEM if k < first else pltpu.HBM) for k in range(len(inputs))]
    if not anywhere:
        specs[0] = pl.BlockSpec(memory_space=pltpu.SMEM)
    return pl.pallas_call(
        kernel,
        out_shape=shapes,
        in_specs=specs,
        out_specs=[pl.BlockSpec(memory_space=pltpu.VMEM)] * len(outs),
        scratch_shapes=[pltpu.VMEM(*one) for one in scratch] + list(semaphores),
        compiler_params=pltpu.CompilerParams(vmem_limit_bytes=max(moved // 2, 8 * 2**20) + held + 4 * 2**20),
        cost_estimate=pl.CostEstimate(flops=flops, bytes_accessed=moved, transcendentals=0),
    )(*inputs)


def sigmoid(value):
    return 0.5 * jnp.tanh(0.5 * value) + 0.5


def silu_grad(value):
    sigma = sigmoid(value)
    return sigma * (1.0 + value * (1.0 - sigma))


def dot(a, b, dims=((1,), (0,))):
    return lax.dot_general(a, b, (dims, ((), ())), preferred_element_type=F32)


def statistics(sums_ref, count, cols):
    mean = sums_ref[0:1, cols] / count
    square = sums_ref[1:2, cols] / count
    return mean, lax.rsqrt(square - mean * mean + EPS)


def col_sum(value):
    return jnp.sum(value, axis=0, keepdims=True)


def octet_sum(value):
    return jnp.sum(value.reshape(value.shape[0] // 8, 8, value.shape[1]), axis=0)


def rows_of(step):
    return pl.ds(pl.multiple_of(step * CHUNK, CHUNK), CHUNK)


def at(index, size):
    if isinstance(index, int):
        return pl.ds(index * size, size)
    return pl.ds(pl.multiple_of(index * size, size), size)


def assemble_kernel(c, plan, me, *refs):
    *parts, out = refs
    number = me[0] * c + me[1]
    for part, masks in zip(parts, plan):
        for a, mask in enumerate(masks):
            other = number ^ mask
            i, j = lax.div(other, c), lax.rem(other, c)
            rows, cols = part.shape[1:]
            out[at(i, rows), at(j, cols)] = part[a]


def assemble_mid_kernel(c, plan, me, *refs):
    parts, outs = refs[: len(plan)], refs[len(plan) :]
    number = me[0] * c + me[1]
    for part, masks in zip(parts, plan):
        for a, mask in enumerate(masks):
            other = number ^ mask
            i, j = lax.div(other, c), lax.rem(other, c)
            rows, cols = part.shape[2:]
            outs[0][:, at(i, rows), at(j, cols)] = part[a, 0:9]
            if len(outs) > 1:
                for k in range(4):
                    outs[1][at(2 * j + k // 2, rows), at(2 * i + k % 2, cols)] = part[a, 9 + k]


def prepare_kernel(c, me, *refs):
    sources, outs, held, arrived = refs[:5], refs[5:-6], refs[-6:-1], refs[-1]
    pieces, (low_in, low_mid, low_head) = outs[:c], outs[c:]
    features, conv_in, conv_mid, conv_out, classifier = held
    order = (1, 0, 2, 3, 4)
    copies = [pltpu.make_async_copy(sources[k], held[k], arrived.at[k]) for k in range(5)]
    for k in order:
        copies[k].start()
    copies[1].wait()
    low_in[...] = conv_in[...].astype(BF16)
    copies[0].wait()
    pixels, images, width = features.shape
    group = images // c
    for t in range(c):
        part = features[:, t * group : (t + 1) * group, :].astype(F32)
        part = part.reshape(pixels * group, width).astype(BF16)
        for k in range(c):

            @pl.when(me[1] == t ^ k)
            def _(part=part, k=k):
                pieces[k][...] = part

    copies[2].wait()
    low_mid[0:9] = conv_mid[...].astype(BF16)
    copies[3].wait()
    if low_mid.shape[0] > 9:
        rows, cols = low_mid.shape[1:]
        for k in range(4):
            part = conv_out[k // 2 * rows : (k // 2 + 1) * rows, k % 2 * cols : (k % 2 + 1) * cols]
            low_mid[9 + k] = part.astype(BF16)
    copies[4].wait()
    tall, classes = classifier.shape
    for k, start in enumerate(range(0, classes, LANES)):
        stop = min(start + LANES, classes)
        rows = slice(k * tall, (k + 1) * tall)
        low_head[rows, 0 : stop - start] = classifier[:, start:stop].astype(BF16)
        if stop - start < LANES:
            low_head[rows, stop - start :] = jnp.zeros((tall, LANES - stop + start), BF16)


def fetch(sources, places, arrived, start=0):
    copies = [pltpu.make_async_copy(x, y, arrived.at[start + k]) for k, (x, y) in enumerate(zip(sources, places))]
    for copy in copies:
        copy.start()
    return copies


def first_kernel(c, me, carried, weights, *refs):
    features, (hidden, sums, held, arrived) = refs[:c], refs[c:]
    chan, depth = me[1], features[0].shape[1]
    width = hidden.shape[1]
    copies = fetch(features, [held.at[k] for k in range(c)], arrived)
    for start in range(0, width, 256):
        cols = slice(start, start + 256)
        value = None
        for k in range(c):
            if start == 0:
                copies[k].wait()
            rows = pl.ds(pl.multiple_of((chan ^ k) * depth, depth), depth)
            term = dot(held[k], weights[rows, cols])
            value = term if value is None else value + term
        hidden[:, cols] = value
        sums[0:1, cols] = col_sum(value)
        sums[1:2, cols] = col_sum(value * value)
    sums[2:, :] = carried[...]


def windows(pad, out, size, group):
    line = size * group
    rows, width = out.shape[0], pad.shape[2]
    for i in range(3):
        for j in range(3):
            tap = 3 * i + j
            out[:, tap * width : (tap + 1) * width] = pad[
                j, i * line : i * line + rows, :
            ].astype(BF16)


def fill(pad, size, group):
    line = size * group
    rows, width = pad.shape[1] - 2 * line, pad.shape[2]
    place = lax.broadcasted_iota(jnp.int32, (rows, 1), 0)
    column = lax.rem(lax.div(place, group), size)
    here = pad[1, line : line + rows, :]
    empty = jnp.zeros((line, width), F32)
    for j in (0, 2):
        moved = pltpu.roll(here, group if j == 0 else rows - group, 0)
        valid = column != (0 if j == 0 else size - 1)
        pad[j, 0:line, :] = empty
        pad[j, line : line + rows, :] = jnp.where(valid, moved, 0.0)
        pad[j, line + rows :, :] = empty


def second_kernel(count, size, group, me, hidden, sums, norms, weights, low_act, out, out_sums, pad, cols):
    rows, width = hidden.shape
    line = size * group
    mean, scale = statistics(sums, count, slice(None))
    gain, shift = norms[0:1, :], norms[1:2, :]
    pad[1, 0:line, :] = jnp.zeros((line, width), F32)
    pad[1, line + rows :, :] = jnp.zeros((line, width), F32)
    for step in range(rows // CHUNK):
        part = slice(step * CHUNK, (step + 1) * CHUNK)
        value = (hidden[part, :] - mean) * scale * gain + shift
        act = (value * sigmoid(value)).astype(BF16)
        low_act[part, :] = act
        pad[1, line + step * CHUNK : line + (step + 1) * CHUNK, :] = act.astype(F32)
    fill(pad, size, group)
    windows(pad, cols, size, group)
    for start in range(0, out.shape[1], 256):
        block = slice(start, start + 256)
        value = dot(cols[...], weights[:, block])
        out[:, block] = value
        out_sums[0:1, block] = col_sum(value)
        out_sums[1:2, block] = col_sum(value * value)


def third_kernel(count, me, hidden, sums, norms, weights, act, out, out_sums):
    mean, scale = statistics(sums, count, slice(None))
    gain, shift = norms[0:1, :], norms[1:2, :]
    for step in range(hidden.shape[0] // CHUNK):
        part = slice(step * CHUNK, (step + 1) * CHUNK)
        value = (hidden[part, :] - mean) * scale * gain + shift
        act[part, :] = (value * sigmoid(value)).astype(BF16)
    for start in range(0, out.shape[1], 256):
        block = slice(start, start + 256)
        value = dot(act[...], weights[:, block])
        out[:, block] = value
        out_sums[0:1, block] = col_sum(value)
        out_sums[1:2, block] = col_sum(value * value)


def head_kernel(count, pixels, group, classes, c, plan, me, hidden, sums, norms, row_weights, target, *refs):
    shards, refs = refs[: len(plan)], refs[len(plan) :]
    sources, (upper, out_sums, packed, loss, features, weights, held, arrived) = refs[:c], refs[c:]
    chan, rows = me[1], hidden.shape[0]
    width = features.shape[2]
    twice = 2 * group
    copies = fetch(sources, [features.at[k] for k in range(c)], arrived)
    number = me[0] * c + chan
    halves = weights.shape[1] // (c * LANES)
    tall = shards[0].shape[1] // halves
    starts, ends = [], []
    for part, masks in zip(shards, plan):
        for a, mask in enumerate(masks):
            other = number ^ mask
            i, j = lax.div(other, c), lax.rem(other, c)
            for k in range(halves):
                starts.append(part.at[a, pl.ds(k * tall, tall), :])
                ends.append(weights.at[at(i, tall), at(j * halves + k, LANES)])
    copies += fetch(starts, ends, arrived, c)
    blocks = [pl.ds(pl.multiple_of((chan ^ k) * width, width), width) for k in range(c)]
    for k, cols in enumerate(blocks):
        mean, scale = statistics(sums, count, cols)
        gain = scale * norms[0:1, cols]
        shift = norms[1:2, cols] - mean * gain
        copies[k].wait()

        def forward(step, pool, k=k, cols=cols, gain=gain, shift=shift):
            part = rows_of(step)
            value = hidden[part, cols] * gain + shift + features[k, part, :].astype(F32)
            sigma = sigmoid(value)
            value = value * sigma
            upper[part, cols] = sigma + value - value * sigma
            return pool + jnp.sum(value.reshape(CHUNK // twice, twice, width), axis=0)

        pool = lax.fori_loop(0, rows // CHUNK, forward, jnp.zeros((twice, width), F32))
        pool = (pool + pltpu.roll(pool, group, 0)) / pixels
        held[:, cols] = pool.astype(BF16)
    depth, space = weights.shape
    for copy in copies[c:]:
        copy.wait()
    pooled = held[...]
    logits = dot(pooled, weights[...])
    column = lax.broadcasted_iota(jnp.int32, logits.shape, 1)
    valid = lax.rem(column, space // c) < classes
    top = jnp.max(jnp.where(valid, logits, -jnp.inf), axis=1, keepdims=True)
    grown = jnp.where(valid, jnp.exp(logits - top), 0.0)
    spread = top + jnp.log(jnp.sum(grown, axis=1, keepdims=True))
    wanted = target[...]
    picked = jnp.sum(wanted * logits, axis=1, keepdims=True)
    weight, share = row_weights[:, 0:1], row_weights[:, 1:2]
    loss[...] = 0.5 * jnp.sum(weight * (spread - picked), axis=0, keepdims=True)
    down = share * (jnp.where(valid, jnp.exp(logits - spread), 0.0) - wanted)
    low_down = down.astype(BF16)
    row = lax.broadcasted_iota(jnp.int32, (twice, 1), 0)
    length = packed.shape[1]
    full = jnp.concatenate([pooled.astype(F32), low_down.astype(F32)], axis=1)
    packed[...] = jnp.where(row < group, full[:, :length], full[:, length:]).astype(BF16)
    for k, cols in enumerate(blocks):
        mean, scale = statistics(sums, count, cols)
        back = dot(low_down, weights[cols, :], ((1,), (1,))) / pixels
        back = jnp.broadcast_to(back[None], (CHUNK // twice, twice, width)).reshape(CHUNK, width)

        def backward(step, so_far, cols=cols, mean=mean, back=back):
            part = rows_of(step)
            value = back * upper[part, cols]
            moved = value * (hidden[part, cols] - mean)
            upper[part, cols] = value
            return (so_far[0] + octet_sum(value), so_far[1] + octet_sum(moved))

        zero = jnp.zeros((8, width), F32)
        first, second = lax.fori_loop(0, rows // CHUNK, backward, (zero, zero))
        out_sums[0:1, cols] = col_sum(first)
        out_sums[1:2, cols] = col_sum(second) * scale
    wide = hidden.shape[1]
    out_sums[:, wide:] = jnp.broadcast_to(loss[...], (2, out_sums.shape[1] - wide))


def lower(upper, hidden, sums, back_sums, norms, count, part, cols):
    mean, scale = statistics(sums, count, cols)
    normed = (hidden[part, cols] - mean) * scale
    slope = scale * norms[0:1, cols]
    return slope * (
        upper[part, cols] - back_sums[0:1, cols] / count - normed * (back_sums[1:2, cols] / count)
    )


def back_three_kernel(
    count, me, upper, hidden, sums, norms, back_sums, weights, hidden_two, sums_two, norms_two, down, out, out_sums
):
    rows, wide = upper.shape
    for start in range(0, wide, 512):
        cols = slice(start, start + 512)
        for step in range(rows // CHUNK):
            part = slice(step * CHUNK, (step + 1) * CHUNK)
            down[part, cols] = lower(
                upper, hidden, sums, back_sums, norms, count, part, cols
            ).astype(BF16)
    for start in range(0, out.shape[1], 256):
        cols = slice(start, start + 256)
        value = dot(down[...], weights[cols, :], ((1,), (1,)))
        finish(value, hidden_two, sums_two, norms_two, count, cols, out, out_sums)


def finish(value, hidden, sums, norms, count, cols, out, out_sums):
    mean, scale = statistics(sums, count, cols)
    normed = (hidden[:, cols] - mean) * scale
    value = value * silu_grad(normed * norms[0:1, cols] + norms[1:2, cols])
    out[:, cols] = value
    out_sums[0:1, cols] = col_sum(value)
    out_sums[1:2, cols] = col_sum(value * normed)


def back_two_kernel(
    count, size, group, me, upper, hidden, sums, norms, back_sums, weights, hidden_one, sums_one, norms_one,
    down, out, out_sums, pad, cols,
):
    rows, width = upper.shape
    line = size * group
    pad[1, 0:line, :] = jnp.zeros((line, width), F32)
    pad[1, line + rows :, :] = jnp.zeros((line, width), F32)
    for step in range(rows // CHUNK):
        part = slice(step * CHUNK, (step + 1) * CHUNK)
        value = lower(upper, hidden, sums, back_sums, norms, count, part, slice(None)).astype(BF16)
        down[part, :] = value
        pad[1, line + step * CHUNK : line + (step + 1) * CHUNK, :] = value.astype(F32)
    fill(pad, size, group)
    windows(pad, cols, size, group)
    for start in range(0, out.shape[1], 256):
        block = slice(start, start + 256)
        value = None
        for tap in range(9):
            base = (8 - tap) * out.shape[1] + start
            term = dot(
                cols[:, tap * width : (tap + 1) * width],
                weights[base : base + 256, :],
                ((1,), (1,)),
            )
            value = term if value is None else value + term
        finish(value, hidden_one, sums_one, norms_one, count, block, out, out_sums)


def spread_blocks(number, c, outs, masks, block):
    for out, row in zip(outs, masks):
        for a, mask in enumerate(row):
            other = number ^ mask
            out[a] = block(lax.div(other, c), lax.rem(other, c))


def turned(value):
    return value.astype(F32).T.astype(BF16)


def grad_mid_kernel(c, masks, size, group, me, act, down, act_two, down_three, *refs):
    *outs, whole, pad, cols, whole_out = refs
    rows, depth = act.shape
    line = size * group
    pad[1, 0:line, :] = jnp.zeros((line, depth), F32)
    pad[1, line + rows :, :] = jnp.zeros((line, depth), F32)
    pad[1, line : line + rows, :] = down[...].astype(F32)
    fill(pad, size, group)
    windows(pad, cols, size, group)
    left = turned(act[...])
    for tap in range(9):
        whole[tap] = dot(left, cols[:, (8 - tap) * depth : (9 - tap) * depth]).astype(BF16)
    left = turned(act_two[...])
    wide = whole_out.shape[1]
    for start in range(0, wide, 512):
        part = slice(start, start + 512)
        whole_out[:, part] = dot(left, down_three[:, part]).astype(BF16)
    height, width = outs[0].shape[2:]
    number = me[0] * c + me[1]
    for out, row in zip(outs, masks):
        for a, mask in enumerate(row):
            other = number ^ mask
            i, j = lax.div(other, c), lax.rem(other, c)
            out[a, 0:9] = whole[:, at(i, height), at(j, width)]
            for k in range(4):
                out[a, 9 + k] = whole_out[at(2 * j + k // 2, height), at(2 * i + k % 2, width)]


def grad_in_kernel(count, c, masks, me, upper, hidden, sums, norms, back_sums, *refs):
    sources, outs, (whole, down, features, arrived) = refs[:c], refs[c:-4], refs[-4:]
    copies = fetch(sources, [features.at[k] for k in range(c)], arrived)
    rows = upper.shape[0]
    for step in range(rows // CHUNK):
        part = slice(step * CHUNK, (step + 1) * CHUNK)
        down[part, :] = lower(
            upper, hidden, sums, back_sums, norms, count, part, slice(None)
        ).astype(BF16)
    depth = features.shape[2]
    for k in range(c):
        copies[k].wait()
        whole[at(me[1] ^ k, depth), :] = dot(features[k], down[...], ((0,), (0,))).astype(BF16)
    height, width = outs[0].shape[1:]
    spread_blocks(
        me[0] * c + me[1], c, outs, masks, lambda i, j: whole[at(i, height), at(j, width)]
    )


def grad_head_kernel(c, tall, space, group, me, *refs):
    *parts, out = refs
    length = parts[0].shape[2]
    wide = 2 * length - c * space
    start = me[0] * tall
    late = start >= length
    row = lax.broadcasted_iota(jnp.int32, (2 * group, 1), 0)
    left, right = [], []
    for part in parts:
        for a in range(part.shape[0]):
            one = part[a, :, at(jnp.where(late, start - length, start) // tall, tall)].astype(F32)
            left.append(jnp.where(late, one, pltpu.roll(one, group, 0)))
            two = part[a, :, at((wide - length) // space + me[1], space)].astype(F32)
            right.append(jnp.where(row < group, 0.0, two))
    left, right = jnp.concatenate(left).astype(BF16), jnp.concatenate(right).astype(BF16)
    out[...] = dot(left, right, ((0,), (0,)))


def add_low(one, other):
    return one + other


def add_quarters_kernel(arrived, own, *outs):
    z = own.shape[0] // 4
    for low, out in enumerate(outs):
        for k in range(z):
            out[k] = add_low(own[low * z + k], arrived[low * z + k])


def add_first_kernel(plan, arrived, own, *outs):
    z = own.shape[0] // 4
    for (start, stop, order), send, keep in zip(plan, outs[0::2], outs[1::2]):
        for low in range(4):
            inside = low // 2 if order[0] == 2 else low % 2
            out = send if low & (order[0] // 2) else keep
            for k in range(z):
                entry = low * z + k
                out[inside * z + k] = add_low(own[entry, start:stop], arrived[entry, start:stop])


def add_second_kernel(*refs):
    parts = len(refs) // 4
    arrived, keeps, outs = refs[:parts], refs[parts : 2 * parts], refs[2 * parts :]
    for one, other, send, keep in zip(arrived, keeps, outs[0::2], outs[1::2]):
        z = send.shape[0]
        for k in range(z):
            keep[k] = add_low(one[k], other[k])
            send[k] = add_low(one[z + k], other[z + k])


def add_third_kernel(plan, *refs):
    parts = len(plan)
    arrived, keeps, outs = refs[:parts], refs[parts : 2 * parts], refs[2 * parts :]
    for (start, stop, _), one, other in zip(plan, arrived, keeps):
        for k, out in enumerate(outs):
            value = one[k].astype(F32) + other[k].astype(F32)
            out[start:stop] = value if k == 0 else value.astype(BF16)


def add_next_kernel(kept, one, two, three, *outs):
    for k, out in enumerate(outs):
        pair = kept[k].astype(F32) + one[k].astype(F32)
        out[...] = (pair + (two[k].astype(F32) + three[k].astype(F32))).astype(out.dtype)


def advance(weight, grad, momentum, average, rate):
    fresh = MOMENTUM * momentum + grad
    weight_new = weight - rate * (grad + MOMENTUM * fresh)
    return (weight_new, fresh, AVERAGE * average + (1.0 - AVERAGE) * weight_new)


def shards(
    d,
    c,
    features,
    labels,
    class_weights,
    conv_in,
    conv_mid,
    conv_out,
    classifier,
    norms,
    momentum_in,
    momentum_mid,
    momentum_out,
    momentum_head,
    momentum_norms,
    average_in,
    average_mid,
    average_out,
    average_head,
    average_norms,
):
    n = d * c
    dp, chan = lax.axis_index("dp"), lax.axis_index("chan")
    number = dp * c + chan
    me = jnp.stack([dp, chan]).astype(jnp.int32)
    images, size = features.shape[0], features.shape[1]
    group = images // c
    pixels = size * size
    count = float(images * pixels * d)
    rows = pixels * group
    deep = features.shape[3]
    mid, wide = conv_in.shape[1] * c, deep * c
    aligned = conv_out.shape[1] % LANES == 0

    fan_in, fan_out = conv_mid.shape[2:]
    classes = classifier.shape[1]
    space = -(-classes // LANES) * LANES
    tall = classifier.shape[0]
    laid = features.transpose(1, 2, 0, 3).reshape(pixels, images, deep)
    narrow_mid = conv_mid.reshape(9, fan_in, fan_out)
    sources = (laid, conv_in, narrow_mid, conv_out, classifier)
    own, mate, other, away, low_in, low_mid, low_head = call(
        functools.partial(prepare_kernel, c),
        [((rows, deep), BF16)] * c
        + [(conv_in.shape, BF16), ((13 if aligned else 9, fan_in, fan_out), BF16)]
        + [((tall * (space // LANES), LANES), BF16)],
        me, *sources, remain=5,
        scratch=[(x.shape, jnp.dtype(x.dtype).type) for x in sources],
        semaphores=[pltpu.SemaphoreType.DMA((5,))],
    )
    if not aligned:
        low_mid = jnp.concatenate([low_mid, conv_out.astype(BF16).reshape(4, fan_in, fan_out)])
    away, other = swap(away, 2, n), swap(other, 2, n)
    high_in = gather_high(low_in, n)
    pieces = [own, swap(mate, 1, n), other, swap(away, 1, n)]
    low_in, side_in = gather_low(high_in, False, n, (away, other))
    high_mid = gather_high(following(low_mid, high_in[1]), n)
    low_mid, side_mid = gather_low(high_mid, True, n, side_in)
    high_head = gather_high(following(low_head, side_mid), n)

    narrow = conv_in.shape[1]
    own = lax.dynamic_index_in_dim(labels.reshape(c, group), chan, 0, keepdims=False)
    own = jnp.concatenate([own, own])
    catalog = lax.broadcasted_iota(jnp.int32, (2 * group, class_weights.shape[0]), 1)
    chosen = catalog == own[:, None]
    weight_row = jnp.sum(jnp.where(chosen, class_weights[None, :], 0), axis=1).astype(F32)
    target = jnp.pad(
        chosen.astype(F32).reshape(2 * group, c, classes), ((0, 0), (0, 0), (0, space - classes))
    ).reshape(2 * group, c * space)
    own_weight = jnp.broadcast_to(0.5 * jnp.sum(weight_row), (1, mid))
    table = jnp.where(dp == 0, norms[:, 0], 0.0)
    table = jnp.where((jnp.arange(c) == chan)[None, :, None], table[:, None, :], 0.0)
    carried = table.reshape(-1, mid)
    own_weight = jnp.concatenate([own_weight, carried])

    def assembled(kernel, parts, *shapes):
        kernel = functools.partial(kernel, c, [masks for _, masks in parts])
        return call(kernel, [(shape, BF16) for shape in shapes], me, *[array for array, _ in parts])

    (whole_in,) = assembled(assemble_kernel, low_in, (wide, mid))
    feature_space = [((c, rows, deep), jnp.bfloat16)]
    feature_ends = [pltpu.SemaphoreType.DMA((c,))]
    hidden_one, sums_one = call(
        functools.partial(first_kernel, c),
        [((rows, mid), F32), ((2 + own_weight.shape[0], mid), F32)], me, own_weight, whole_in, *pieces,
        flops=2 * rows * wide * mid, scratch=feature_space, semaphores=feature_ends, remain=c,
    )
    sums_one, *_ = total(sums_one, n)
    weight_sum = sums_one[2, 0]
    tables = sums_one[3:].reshape(2, c, -1)
    norms_one = tables[:, :, :narrow].reshape(2, mid)
    norms_two = tables[:, :, narrow : 2 * narrow].reshape(2, mid)
    norms_three = tables[:, :, 2 * narrow :].reshape(2, wide)

    if aligned:
        whole_mid, whole_out = assembled(assemble_mid_kernel, low_mid, (9, mid, mid), (mid, wide))
    else:
        (whole_mid,) = assembled(assemble_mid_kernel, low_mid, (9, mid, mid))
        blocks = jnp.concatenate([array[:, 9:] for array, _ in low_mid])
        order = jnp.array([mask for _, masks in low_mid for mask in masks])
        blocks = jnp.take(blocks, jnp.argsort(order ^ number), axis=0)
        blocks = blocks.reshape((d, c) + conv_out.shape)
        whole_out = blocks.transpose(1, 2, 0, 3).reshape(mid, wide)
    whole_mid = whole_mid.reshape(9 * mid, mid)
    line = size * group
    padded = ((3, rows + 2 * line, mid), jnp.float32)
    many = ((rows, 9 * mid), jnp.bfloat16)
    act_one, hidden_two, sums_two = call(
        functools.partial(second_kernel, count, size, group),
        [((rows, mid), BF16), ((rows, mid), F32), ((2, mid), F32)],
        me, hidden_one, sums_one, norms_one, whole_mid,
        flops=18 * rows * mid * mid, scratch=[padded, many],
    )
    stack_head = following(jnp.stack(high_head), [low_mid[3][0], low_mid[4][0]])
    near_head, side_head = swap(stack_head, 2, n), swap(stack_head, 4, n)
    sums_two, middle_two = total(sums_two, n)
    hidden_two = following(hidden_two, (near_head, side_head))

    act_two, hidden_three, sums_three = call(
        functools.partial(third_kernel, count),
        [((rows, mid), BF16), ((rows, wide), F32), ((2, wide), F32)],
        me, hidden_two, sums_two, norms_two, whole_out,
        flops=2 * rows * mid * wide,
    )
    sums_three, middle_three = total(sums_three, n)
    low_head = gather_cross(stack_head, near_head, side_head, n, middle_two)

    row_weights = jnp.stack([weight_row, weight_row / weight_sum], axis=1)
    upper_three, back_three, packed, _ = call(
        functools.partial(head_kernel, count, pixels, group, classes, c, [masks for _, masks in low_head]),
        [((rows, wide), F32), ((2, wide + LANES), F32), ((2 * group, (wide + c * space) // 2), BF16), ((1, 1), F32)],
        me, hidden_three, sums_three, norms_three, row_weights, target, *[array for array, _ in low_head], *pieces,
        flops=4 * 8 * wide * c * space, remain=len(low_head) + c,
        scratch=feature_space + [((wide, c * space), jnp.bfloat16), ((2 * group, wide), jnp.bfloat16)],
        semaphores=[pltpu.SemaphoreType.DMA((c + n * (space // LANES),))],
    )
    back_three, *_ = total(back_three, n)
    loss_sum = back_three[0, wide]

    down_three, upper_two, back_two = call(
        functools.partial(back_three_kernel, count),
        [((rows, wide), BF16), ((rows, mid), F32), ((2, mid), F32)],
        me, upper_three, hidden_three, sums_three, norms_three, back_three, whole_out,
        hidden_two, sums_two, norms_two,
        flops=2 * rows * mid * wide,
    )
    def blocks_of(shape):
        return [((n // 2,) + shape, BF16)] * 2

    masks = slot_masks(n)
    back_two, *_ = total(back_two, n)

    down_two, upper_one, back_one = call(
        functools.partial(back_two_kernel, count, size, group),
        [((rows, mid), BF16), ((rows, mid), F32), ((2, mid), F32)],
        me, upper_two, hidden_two, sums_two, norms_two, back_two, whole_mid,
        hidden_one, sums_one, norms_one,
        flops=18 * rows * mid * mid, scratch=[padded, many],
    )

    back_one = back_one + swap(back_one, 1, n)
    down_two = following(down_two, back_one)
    if aligned:
        parts_mid = call(
            functools.partial(grad_mid_kernel, c, masks, size, group), blocks_of((13, fan_in, fan_out)),
            me, act_one, down_two, act_two, down_three, flops=18 * rows * mid * mid,
            scratch=[((9, mid, mid), jnp.bfloat16), padded, many, ((mid, wide), jnp.bfloat16)],
        )
    else:
        pad = jnp.pad(act_one.reshape(size, size, group, mid), ((1, 1), (1, 1), (0, 0), (0, 0)))
        whole = [
            dot(pad[i : i + size, j : j + size].reshape(rows, mid), down_two, ((0,), (0,))).astype(BF16)
            for i in range(3)
            for j in range(3)
        ]
        whole = jnp.stack(whole).reshape(9, d, fan_in, c, fan_out).transpose(1, 3, 0, 2, 4)
        whole_two = dot(act_two, down_three, ((0,), (0,))).astype(BF16)
        whole_two = whole_two.reshape((c, conv_out.shape[0], d, conv_out.shape[1])).transpose(2, 0, 1, 3)
        whole_two = whole_two.reshape(d, c, 4, fan_in, fan_out)
        whole = jnp.concatenate([whole, whole_two], axis=2).reshape(n, 13, fan_in, fan_out)
        parts_mid = [jnp.take(whole, jnp.array(row) ^ number, axis=0) for row in masks]
    plan = [(0, 7, (4, 2)), (7, 13, (2, 4))]
    sends, keeps = split_start(*parts_mid, plan, n)
    back_one, half_way = total(back_one, n, sends[0], True)
    sends = following(sends, half_way)
    arrived = [swap(send, order[0], n) for send, (_, _, order) in zip(sends, plan)]
    sends, keeps = split_second(arrived, keeps, n)
    upper_one = following(upper_one, sends)
    parts_in = call(
        functools.partial(grad_in_kernel, count, c, masks), blocks_of(conv_in.shape),
        me, upper_one, hidden_one, sums_one, norms_one, back_one, *pieces,
        flops=2 * rows * mid * wide, remain=c, semaphores=feature_ends,
        scratch=[((wide, mid), jnp.bfloat16), ((rows, mid), jnp.bfloat16)] + feature_space,
    )
    arrived = [swap(send, order[1], n) for send, (_, _, order) in zip(sends, plan)]
    kept_in, *sends_in = scatter_start(*parts_in, n)
    sums_mid = split_third(arrived, keeps, plan, n)
    last_mid = scatter_last(sums_mid, n)
    arrived_in = [swap(send, mask, n) for send, mask in zip(sends_in, (2, 4, 6))]
    arrived_in, last_mid = lax.optimization_barrier((arrived_in, last_mid))
    sums_in = scatter_next(kept_in, arrived_in, n)
    last_mid = following(last_mid, sums_in[0])
    grad_mid = added(last_mid)
    grad_mid, grad_out = grad_mid[:9].reshape(conv_mid.shape), grad_mid[9:]
    if aligned:
        grad_out = grad_out.reshape(2, 2, fan_in, fan_out).transpose(0, 2, 1, 3)
    grad_out = grad_out.reshape(conv_out.shape)
    grad_in = added(scatter_last(sums_in, n))

    pairs, _ = gather_low(gather_high(packed, n), False, n)
    pairs = [(array, masks) for array, (_, masks) in zip(following([array for array, _ in pairs], sums_in[0]), pairs)]
    if aligned:
        (grad_head,) = call(
            functools.partial(grad_head_kernel, c, tall, space, group), [((tall, space), F32)],
            me, *[array for array, _ in pairs],
        )
    else:
        everything = jnp.concatenate([array for array, _ in pairs])
        everything = jnp.concatenate([everything[:, :group], everything[:, group:]], axis=2)
        everything = everything.reshape(-1, wide + c * space)
        pooled = lax.dynamic_slice_in_dim(everything, dp * tall, tall, axis=1)
        upper_logits = lax.dynamic_slice_in_dim(everything, wide + chan * space, space, axis=1)
        grad_head = dot(pooled, upper_logits, ((0,), (0,)))
    grad_head = grad_head[:, :classes]

    def mine(sums, width):
        return lax.dynamic_slice_in_dim(sums[:2], chan * width, width, axis=1)[::-1]

    grad_norms = jnp.concatenate(
        [mine(back_one, narrow), mine(back_two, narrow), mine(back_three, deep)], axis=1
    )[:, None, :]
    params = (conv_in, conv_mid, conv_out, classifier, norms)
    grads = (grad_in, grad_mid, grad_out, grad_head, grad_norms)
    moments = (momentum_in, momentum_mid, momentum_out, momentum_head, momentum_norms)
    averages = (average_in, average_mid, average_out, average_head, average_norms)
    rates = (RATE_MATRIX, RATE_MATRIX, RATE_MATRIX, RATE_MATRIX, RATE_NORM)
    results = [
        advance(p, g, m, a, r) for p, g, m, a, r in zip(params, grads, moments, averages, rates)
    ]
    news = [item[0] for item in results]
    freshs = [item[1] for item in results]
    means = [item[2] for item in results]
    copies = [item.astype(BF16) for item in news]
    return (loss_sum, weight_sum, *news, *freshs, *means, *copies)


def solution(mesh):
    matrices = (P("dp", "chan"), P(None, None, "dp", "chan"), P("chan", "dp"), P("dp", "chan"), P(None, "chan", None))
    return jax.shard_map(
        functools.partial(shards, mesh.shape["dp"], mesh.shape["chan"]),
        mesh=mesh,
        in_specs=(P("dp", None, None, "chan"), P("dp"), P()) + matrices * 3,
        out_specs=(P(), P()) + matrices * 4,
        check_vma=False,
    )
```

```python
import functools
import math

import jax
import jax.numpy as jnp
from jax import lax
from jax.experimental import pallas as pl
from jax.experimental.pallas import tpu as pltpu
from jax.sharding import PartitionSpec as P

EPS = 1e-05
MOMENTUM = 0.5
AVERAGE = 0.5
RATE_MATRIX = 16.0
RATE_NORM = 64.0
AXES = ("dp", "chan")
F32 = jnp.float32
BF16 = jnp.bfloat16
CHUNK = 80
LANES = 128


def swap(array, mask, n):
    return lax.ppermute(array, AXES, [(d, d ^ mask) for d in range(n)])


def tree_sum(parts):
    while len(parts) > 1:
        parts = [parts[k] + parts[k + 1] for k in range(0, len(parts), 2)]
    return parts[0]


def high_masks(n):
    return [8 * k for k in range(n // 8)]


def total(array, n, late=None, paired=False):
    pair = array if paired else array + swap(array, 1, n)
    array = tree_sum([pair] + [swap(pair, mask, n) for mask in (2, 4, 6)])
    array = following(array, late)
    return tree_sum([array] + [swap(array, mask, n) for mask in high_masks(n)[1:]]), array


def following(value, earlier):
    return value if earlier is None else lax.optimization_barrier((value, earlier))[0]


def gather_high(shard, n):
    return [shard] + [swap(shard, mask, n) for mask in high_masks(n)[1:]]


def gather_low(parts, halves, n, after=None):
    stack = following(jnp.stack(parts), after)
    near, side = swap(stack, 2, n), swap(stack, 4, n)
    if halves:
        return gather_cross(stack, near, side, n), side
    masks = high_masks(n)
    pairs = list(zip((stack, side, near, swap(stack, 6, n)), ([m ^ low for m in masks] for low in (0, 4, 2, 6))))
    return pairs + [(swap(array, 1, n), [m ^ 1 for m in row]) for array, row in pairs], side


def gather_cross(stack, near, side, n, after=None):
    masks = high_masks(n)
    half = len(masks) // 2
    first, second = following((near[:half], side[half:]), after)
    pairs = [(stack, masks), (side, [m ^ 4 for m in masks]), (near, [m ^ 2 for m in masks])]
    pairs.append((swap(first, 4, n), [m ^ 6 for m in masks[:half]]))
    pairs.append((swap(second, 2, n), [m ^ 6 for m in masks[half:]]))
    return pairs + [(swap(array, 1, n), [m ^ 1 for m in row]) for array, row in pairs]


def slot_masks(n):
    return [[core ^ low ^ high for low in (0, 2, 4, 6) for high in high_masks(n)] for core in (0, 1)]


def scatter_start(own, other, n):
    outs = [((n // 8,) + own.shape[1:], BF16)] * 4
    return call(add_quarters_kernel, outs, swap(other, 1, n), own, anywhere=True)


def scatter_next(kept, arrived, n):
    shape = kept.shape[1:]
    outs = [(shape, F32)] + [(shape, BF16)] * (n // 8 - 1)
    return call(add_next_kernel, outs, kept, *arrived, anywhere=True)


def split_start(own, other, plan, n):
    shape = own.shape[1:]
    halves = [((n // 4, stop - start) + shape[1:], BF16) for start, stop, _ in plan for _ in (0, 1)]
    outs = call(functools.partial(add_first_kernel, plan), halves, swap(other, 1, n), own, anywhere=True)
    return outs[0::2], outs[1::2]


def split_second(arrived, keeps, n):
    quarters = [((n // 8,) + keep.shape[1:], BF16) for keep in keeps for _ in (0, 1)]
    outs = call(add_second_kernel, quarters, *arrived, *keeps, anywhere=True)
    return outs[0::2], outs[1::2]


def split_third(arrived, keeps, plan, n):
    shape = (plan[-1][1],) + keeps[0].shape[2:]
    outs = [(shape, F32)] + [(shape, BF16)] * (n // 8 - 1)
    return call(functools.partial(add_third_kernel, plan), outs, *arrived, *keeps, anywhere=True)


def scatter_last(sums, n):
    return [sums[0]] + [swap(part, mask, n) for part, mask in zip(sums[1:], high_masks(n)[1:])]


def added(parts):
    return tree_sum([part.astype(F32) for part in parts])


def call(kernel, outs, *inputs, flops=0, anywhere=False, scratch=(), semaphores=(), remain=0):
    first = len(inputs) - remain
    inputs = [pltpu.with_memory_space_constraint(x, pltpu.HBM) if k >= first else x for k, x in enumerate(inputs)]
    moved = sum(x.size * x.dtype.itemsize for x in inputs)
    shapes = [jax.ShapeDtypeStruct(*out) for out in outs]
    moved += sum(s.size * s.dtype.itemsize for s in shapes)
    held = sum(math.prod(shape) * dtype(0).itemsize for shape, dtype in scratch)
    specs = [pl.BlockSpec(memory_space=pltpu.VMEM if k < first else pltpu.HBM) for k in range(len(inputs))]
    if not anywhere:
        specs[0] = pl.BlockSpec(memory_space=pltpu.SMEM)
    return pl.pallas_call(
        kernel,
        out_shape=shapes,
        in_specs=specs,
        out_specs=[pl.BlockSpec(memory_space=pltpu.VMEM)] * len(outs),
        scratch_shapes=[pltpu.VMEM(*one) for one in scratch] + list(semaphores),
        compiler_params=pltpu.CompilerParams(vmem_limit_bytes=max(moved // 2, 8 * 2**20) + held + 4 * 2**20),
        cost_estimate=pl.CostEstimate(flops=flops, bytes_accessed=moved, transcendentals=0),
    )(*inputs)


def sigmoid(value):
    return 0.5 * jnp.tanh(0.5 * value) + 0.5


def silu_grad(value):
    sigma = sigmoid(value)
    return sigma * (1.0 + value * (1.0 - sigma))


def dot(a, b, dims=((1,), (0,))):
    return lax.dot_general(a, b, (dims, ((), ())), preferred_element_type=F32)


def statistics(sums_ref, count, cols):
    mean = sums_ref[0:1, cols] / count
    square = sums_ref[1:2, cols] / count
    return mean, lax.rsqrt(square - mean * mean + EPS)


def col_sum(value):
    return jnp.sum(value, axis=0, keepdims=True)


def octet_sum(value):
    return jnp.sum(value.reshape(value.shape[0] // 8, 8, value.shape[1]), axis=0)


def rows_of(step):
    return pl.ds(pl.multiple_of(step * CHUNK, CHUNK), CHUNK)


def at(index, size):
    if isinstance(index, int):
        return pl.ds(index * size, size)
    return pl.ds(pl.multiple_of(index * size, size), size)


def assemble_kernel(c, plan, me, *refs):
    *parts, out = refs
    number = me[0] * c + me[1]
    for part, masks in zip(parts, plan):
        for a, mask in enumerate(masks):
            other = number ^ mask
            i, j = lax.div(other, c), lax.rem(other, c)
            rows, cols = part.shape[1:]
            out[at(i, rows), at(j, cols)] = part[a]


def assemble_mid_kernel(c, plan, me, *refs):
    parts, outs = refs[: len(plan)], refs[len(plan) :]
    number = me[0] * c + me[1]
    for part, masks in zip(parts, plan):
        for a, mask in enumerate(masks):
            other = number ^ mask
            i, j = lax.div(other, c), lax.rem(other, c)
            rows, cols = part.shape[2:]
            outs[0][:, at(i, rows), at(j, cols)] = part[a, 0:9]
            if len(outs) > 1:
                for k in range(4):
                    outs[1][at(2 * j + k // 2, rows), at(2 * i + k % 2, cols)] = part[a, 9 + k]


def prepare_kernel(c, me, *refs):
    sources, outs, held, arrived = refs[:5], refs[5:-6], refs[-6:-1], refs[-1]
    pieces, (low_in, low_mid, low_head) = outs[:c], outs[c:]
    features, conv_in, conv_mid, conv_out, classifier = held
    order = (1, 0, 2, 3, 4)
    copies = [pltpu.make_async_copy(sources[k], held[k], arrived.at[k]) for k in range(5)]
    for k in order:
        copies[k].start()
    copies[1].wait()
    low_in[...] = conv_in[...].astype(BF16)
    copies[0].wait()
    pixels, images, width = features.shape
    group = images // c
    for t in range(c):
        part = features[:, t * group : (t + 1) * group, :].astype(F32)
        part = part.reshape(pixels * group, width).astype(BF16)
        for k in range(c):

            @pl.when(me[1] == t ^ k)
            def _(part=part, k=k):
                pieces[k][...] = part

    copies[2].wait()
    low_mid[0:9] = conv_mid[...].astype(BF16)
    copies[3].wait()
    if low_mid.shape[0] > 9:
        rows, cols = low_mid.shape[1:]
        for k in range(4):
            part = conv_out[k // 2 * rows : (k // 2 + 1) * rows, k % 2 * cols : (k % 2 + 1) * cols]
            low_mid[9 + k] = part.astype(BF16)
    copies[4].wait()
    tall, classes = classifier.shape
    for k, start in enumerate(range(0, classes, LANES)):
        stop = min(start + LANES, classes)
        rows = slice(k * tall, (k + 1) * tall)
        low_head[rows, 0 : stop - start] = classifier[:, start:stop].astype(BF16)
        if stop - start < LANES:
            low_head[rows, stop - start :] = jnp.zeros((tall, LANES - stop + start), BF16)


def fetch(sources, places, arrived, start=0):
    copies = [pltpu.make_async_copy(x, y, arrived.at[start + k]) for k, (x, y) in enumerate(zip(sources, places))]
    for copy in copies:
        copy.start()
    return copies


def first_kernel(c, me, carried, weights, *refs):
    features, (hidden, sums, held, arrived) = refs[:c], refs[c:]
    chan, depth = me[1], features[0].shape[1]
    width = hidden.shape[1]
    copies = fetch(features, [held.at[k] for k in range(c)], arrived)
    for start in range(0, width, 256):
        cols = slice(start, start + 256)
        value = None
        for k in range(c):
            if start == 0:
                copies[k].wait()
            rows = pl.ds(pl.multiple_of((chan ^ k) * depth, depth), depth)
            term = dot(held[k], weights[rows, cols])
            value = term if value is None else value + term
        hidden[:, cols] = value
        sums[0:1, cols] = col_sum(value)
        sums[1:2, cols] = col_sum(value * value)
    sums[2:, :] = carried[...]


def windows(pad, out, size, group):
    line = size * group
    rows, width = out.shape[0], pad.shape[2]
    for i in range(3):
        for j in range(3):
            tap = 3 * i + j
            out[:, tap * width : (tap + 1) * width] = pad[
                j, i * line : i * line + rows, :
            ].astype(BF16)


def fill(pad, size, group):
    line = size * group
    rows, width = pad.shape[1] - 2 * line, pad.shape[2]
    place = lax.broadcasted_iota(jnp.int32, (rows, 1), 0)
    column = lax.rem(lax.div(place, group), size)
    here = pad[1, line : line + rows, :]
    empty = jnp.zeros((line, width), F32)
    for j in (0, 2):
        moved = pltpu.roll(here, group if j == 0 else rows - group, 0)
        valid = column != (0 if j == 0 else size - 1)
        pad[j, 0:line, :] = empty
        pad[j, line : line + rows, :] = jnp.where(valid, moved, 0.0)
        pad[j, line + rows :, :] = empty


def second_kernel(count, size, group, me, hidden, sums, norms, weights, low_act, out, out_sums, pad, cols):
    rows, width = hidden.shape
    line = size * group
    mean, scale = statistics(sums, count, slice(None))
    gain, shift = norms[0:1, :], norms[1:2, :]
    pad[1, 0:line, :] = jnp.zeros((line, width), F32)
    pad[1, line + rows :, :] = jnp.zeros((line, width), F32)
    for step in range(rows // CHUNK):
        part = slice(step * CHUNK, (step + 1) * CHUNK)
        value = (hidden[part, :] - mean) * scale * gain + shift
        act = (value * sigmoid(value)).astype(BF16)
        low_act[part, :] = act
        pad[1, line + step * CHUNK : line + (step + 1) * CHUNK, :] = act.astype(F32)
    fill(pad, size, group)
    windows(pad, cols, size, group)
    for start in range(0, out.shape[1], 256):
        block = slice(start, start + 256)
        value = dot(cols[...], weights[:, block])
        out[:, block] = value
        out_sums[0:1, block] = col_sum(value)
        out_sums[1:2, block] = col_sum(value * value)


def third_kernel(count, me, hidden, sums, norms, weights, act, out, out_sums):
    mean, scale = statistics(sums, count, slice(None))
    gain, shift = norms[0:1, :], norms[1:2, :]
    for step in range(hidden.shape[0] // CHUNK):
        part = slice(step * CHUNK, (step + 1) * CHUNK)
        value = (hidden[part, :] - mean) * scale * gain + shift
        act[part, :] = (value * sigmoid(value)).astype(BF16)
    for start in range(0, out.shape[1], 256):
        block = slice(start, start + 256)
        value = dot(act[...], weights[:, block])
        out[:, block] = value
        out_sums[0:1, block] = col_sum(value)
        out_sums[1:2, block] = col_sum(value * value)


def head_kernel(count, pixels, group, classes, c, plan, me, hidden, sums, norms, row_weights, target, *refs):
    shards, refs = refs[: len(plan)], refs[len(plan) :]
    sources, (upper, out_sums, packed, loss, features, weights, held, arrived) = refs[:c], refs[c:]
    chan, rows = me[1], hidden.shape[0]
    width = features.shape[2]
    twice = 2 * group
    copies = fetch(sources, [features.at[k] for k in range(c)], arrived)
    number = me[0] * c + chan
    halves = weights.shape[1] // (c * LANES)
    tall = shards[0].shape[1] // halves
    starts, ends = [], []
    for part, masks in zip(shards, plan):
        for a, mask in enumerate(masks):
            other = number ^ mask
            i, j = lax.div(other, c), lax.rem(other, c)
            for k in range(halves):
                starts.append(part.at[a, pl.ds(k * tall, tall), :])
                ends.append(weights.at[at(i, tall), at(j * halves + k, LANES)])
    copies += fetch(starts, ends, arrived, c)
    blocks = [pl.ds(pl.multiple_of((chan ^ k) * width, width), width) for k in range(c)]
    for k, cols in enumerate(blocks):
        mean, scale = statistics(sums, count, cols)
        gain = scale * norms[0:1, cols]
        shift = norms[1:2, cols] - mean * gain
        copies[k].wait()

        def forward(step, pool, k=k, cols=cols, gain=gain, shift=shift):
            part = rows_of(step)
            value = hidden[part, cols] * gain + shift + features[k, part, :].astype(F32)
            sigma = sigmoid(value)
            value = value * sigma
            upper[part, cols] = sigma + value - value * sigma
            return pool + jnp.sum(value.reshape(CHUNK // twice, twice, width), axis=0)

        pool = lax.fori_loop(0, rows // CHUNK, forward, jnp.zeros((twice, width), F32))
        pool = (pool + pltpu.roll(pool, group, 0)) / pixels
        held[:, cols] = pool.astype(BF16)
    depth, space = weights.shape
    for copy in copies[c:]:
        copy.wait()
    pooled = held[...]
    logits = dot(pooled, weights[...])
    column = lax.broadcasted_iota(jnp.int32, logits.shape, 1)
    valid = lax.rem(column, space // c) < classes
    top = jnp.max(jnp.where(valid, logits, -jnp.inf), axis=1, keepdims=True)
    grown = jnp.where(valid, jnp.exp(logits - top), 0.0)
    spread = top + jnp.log(jnp.sum(grown, axis=1, keepdims=True))
    wanted = target[...]
    picked = jnp.sum(wanted * logits, axis=1, keepdims=True)
    weight, share = row_weights[:, 0:1], row_weights[:, 1:2]
    loss[...] = 0.5 * jnp.sum(weight * (spread - picked), axis=0, keepdims=True)
    down = share * (jnp.where(valid, jnp.exp(logits - spread), 0.0) - wanted)
    low_down = down.astype(BF16)
    row = lax.broadcasted_iota(jnp.int32, (twice, 1), 0)
    length = packed.shape[1]
    full = jnp.concatenate([pooled.astype(F32), low_down.astype(F32)], axis=1)
    packed[...] = jnp.where(row < group, full[:, :length], full[:, length:]).astype(BF16)
    for k, cols in enumerate(blocks):
        mean, scale = statistics(sums, count, cols)
        back = dot(low_down, weights[cols, :], ((1,), (1,))) / pixels
        back = jnp.broadcast_to(back[None], (CHUNK // twice, twice, width)).reshape(CHUNK, width)

        def backward(step, so_far, cols=cols, mean=mean, back=back):
            part = rows_of(step)
            value = back * upper[part, cols]
            moved = value * (hidden[part, cols] - mean)
            upper[part, cols] = value
            return (so_far[0] + octet_sum(value), so_far[1] + octet_sum(moved))

        zero = jnp.zeros((8, width), F32)
        first, second = lax.fori_loop(0, rows // CHUNK, backward, (zero, zero))
        out_sums[0:1, cols] = col_sum(first)
        out_sums[1:2, cols] = col_sum(second) * scale
    wide = hidden.shape[1]
    out_sums[:, wide:] = jnp.broadcast_to(loss[...], (2, out_sums.shape[1] - wide))


def lower(upper, hidden, sums, back_sums, norms, count, part, cols):
    mean, scale = statistics(sums, count, cols)
    normed = (hidden[part, cols] - mean) * scale
    slope = scale * norms[0:1, cols]
    return slope * (
        upper[part, cols] - back_sums[0:1, cols] / count - normed * (back_sums[1:2, cols] / count)
    )


def back_three_kernel(
    count, me, upper, hidden, sums, norms, back_sums, weights, hidden_two, sums_two, norms_two, down, out, out_sums
):
    rows, wide = upper.shape
    for start in range(0, wide, 512):
        cols = slice(start, start + 512)
        for step in range(rows // CHUNK):
            part = slice(step * CHUNK, (step + 1) * CHUNK)
            down[part, cols] = lower(
                upper, hidden, sums, back_sums, norms, count, part, cols
            ).astype(BF16)
    for start in range(0, out.shape[1], 256):
        cols = slice(start, start + 256)
        value = dot(down[...], weights[cols, :], ((1,), (1,)))
        finish(value, hidden_two, sums_two, norms_two, count, cols, out, out_sums)


def finish(value, hidden, sums, norms, count, cols, out, out_sums):
    mean, scale = statistics(sums, count, cols)
    normed = (hidden[:, cols] - mean) * scale
    value = value * silu_grad(normed * norms[0:1, cols] + norms[1:2, cols])
    out[:, cols] = value
    out_sums[0:1, cols] = col_sum(value)
    out_sums[1:2, cols] = col_sum(value * normed)


def back_two_kernel(
    count, size, group, me, upper, hidden, sums, norms, back_sums, weights, hidden_one, sums_one, norms_one,
    down, out, out_sums, pad, cols,
):
    rows, width = upper.shape
    line = size * group
    pad[1, 0:line, :] = jnp.zeros((line, width), F32)
    pad[1, line + rows :, :] = jnp.zeros((line, width), F32)
    for step in range(rows // CHUNK):
        part = slice(step * CHUNK, (step + 1) * CHUNK)
        value = lower(upper, hidden, sums, back_sums, norms, count, part, slice(None)).astype(BF16)
        down[part, :] = value
        pad[1, line + step * CHUNK : line + (step + 1) * CHUNK, :] = value.astype(F32)
    fill(pad, size, group)
    windows(pad, cols, size, group)
    for start in range(0, out.shape[1], 256):
        block = slice(start, start + 256)
        value = None
        for tap in range(9):
            base = (8 - tap) * out.shape[1] + start
            term = dot(
                cols[:, tap * width : (tap + 1) * width],
                weights[base : base + 256, :],
                ((1,), (1,)),
            )
            value = term if value is None else value + term
        finish(value, hidden_one, sums_one, norms_one, count, block, out, out_sums)


def spread_blocks(number, c, outs, masks, block):
    for out, row in zip(outs, masks):
        for a, mask in enumerate(row):
            other = number ^ mask
            out[a] = block(lax.div(other, c), lax.rem(other, c))


def turned(value):
    return value.astype(F32).T.astype(BF16)


def grad_mid_kernel(c, masks, size, group, me, act, down, act_two, down_three, *refs):
    *outs, whole, pad, cols, whole_out = refs
    rows, depth = act.shape
    line = size * group
    pad[1, 0:line, :] = jnp.zeros((line, depth), F32)
    pad[1, line + rows :, :] = jnp.zeros((line, depth), F32)
    pad[1, line : line + rows, :] = down[...].astype(F32)
    fill(pad, size, group)
    windows(pad, cols, size, group)
    left = turned(act[...])
    for tap in range(9):
        whole[tap] = dot(left, cols[:, (8 - tap) * depth : (9 - tap) * depth]).astype(BF16)
    left = turned(act_two[...])
    wide = whole_out.shape[1]
    for start in range(0, wide, 512):
        part = slice(start, start + 512)
        whole_out[:, part] = dot(left, down_three[:, part]).astype(BF16)
    height, width = outs[0].shape[2:]
    number = me[0] * c + me[1]
    for out, row in zip(outs, masks):
        for a, mask in enumerate(row):
            other = number ^ mask
            i, j = lax.div(other, c), lax.rem(other, c)
            out[a, 0:9] = whole[:, at(i, height), at(j, width)]
            for k in range(4):
                out[a, 9 + k] = whole_out[at(2 * j + k // 2, height), at(2 * i + k % 2, width)]


def grad_in_kernel(count, c, masks, me, upper, hidden, sums, norms, back_sums, *refs):
    sources, outs, (whole, down, features, arrived) = refs[:c], refs[c:-4], refs[-4:]
    copies = fetch(sources, [features.at[k] for k in range(c)], arrived)
    rows = upper.shape[0]
    for step in range(rows // CHUNK):
        part = slice(step * CHUNK, (step + 1) * CHUNK)
        down[part, :] = lower(
            upper, hidden, sums, back_sums, norms, count, part, slice(None)
        ).astype(BF16)
    depth = features.shape[2]
    for k in range(c):
        copies[k].wait()
        whole[at(me[1] ^ k, depth), :] = dot(features[k], down[...], ((0,), (0,))).astype(BF16)
    height, width = outs[0].shape[1:]
    spread_blocks(
        me[0] * c + me[1], c, outs, masks, lambda i, j: whole[at(i, height), at(j, width)]
    )


def grad_head_kernel(c, tall, space, group, me, *refs):
    *parts, out = refs
    length = parts[0].shape[2]
    wide = 2 * length - c * space
    start = me[0] * tall
    late = start >= length
    row = lax.broadcasted_iota(jnp.int32, (2 * group, 1), 0)
    left, right = [], []
    for part in parts:
        for a in range(part.shape[0]):
            one = part[a, :, at(jnp.where(late, start - length, start) // tall, tall)].astype(F32)
            left.append(jnp.where(late, one, pltpu.roll(one, group, 0)))
            two = part[a, :, at((wide - length) // space + me[1], space)].astype(F32)
            right.append(jnp.where(row < group, 0.0, two))
    left, right = jnp.concatenate(left).astype(BF16), jnp.concatenate(right).astype(BF16)
    out[...] = dot(left, right, ((0,), (0,)))


def add_low(one, other):
    return one + other


def add_quarters_kernel(arrived, own, *outs):
    z = own.shape[0] // 4
    for low, out in enumerate(outs):
        for k in range(z):
            out[k] = add_low(own[low * z + k], arrived[low * z + k])


def add_first_kernel(plan, arrived, own, *outs):
    z = own.shape[0] // 4
    for (start, stop, order), send, keep in zip(plan, outs[0::2], outs[1::2]):
        for low in range(4):
            inside = low // 2 if order[0] == 2 else low % 2
            out = send if low & (order[0] // 2) else keep
            for k in range(z):
                entry = low * z + k
                out[inside * z + k] = add_low(own[entry, start:stop], arrived[entry, start:stop])


def add_second_kernel(*refs):
    parts = len(refs) // 4
    arrived, keeps, outs = refs[:parts], refs[parts : 2 * parts], refs[2 * parts :]
    for one, other, send, keep in zip(arrived, keeps, outs[0::2], outs[1::2]):
        z = send.shape[0]
        for k in range(z):
            keep[k] = add_low(one[k], other[k])
            send[k] = add_low(one[z + k], other[z + k])


def add_third_kernel(plan, *refs):
    parts = len(plan)
    arrived, keeps, outs = refs[:parts], refs[parts : 2 * parts], refs[2 * parts :]
    for (start, stop, _), one, other in zip(plan, arrived, keeps):
        for k, out in enumerate(outs):
            value = one[k].astype(F32) + other[k].astype(F32)
            out[start:stop] = value if k == 0 else value.astype(BF16)


def add_next_kernel(kept, one, two, three, *outs):
    for k, out in enumerate(outs):
        pair = kept[k].astype(F32) + one[k].astype(F32)
        out[...] = (pair + (two[k].astype(F32) + three[k].astype(F32))).astype(out.dtype)


def advance(weight, grad, momentum, average, rate):
    fresh = MOMENTUM * momentum + grad
    weight_new = weight - rate * (grad + MOMENTUM * fresh)
    return (weight_new, fresh, AVERAGE * average + (1.0 - AVERAGE) * weight_new)


def shards(
    d,
    c,
    features,
    labels,
    class_weights,
    conv_in,
    conv_mid,
    conv_out,
    classifier,
    norms,
    momentum_in,
    momentum_mid,
    momentum_out,
    momentum_head,
    momentum_norms,
    average_in,
    average_mid,
    average_out,
    average_head,
    average_norms,
):
    n = d * c
    dp, chan = lax.axis_index("dp"), lax.axis_index("chan")
    number = dp * c + chan
    me = jnp.stack([dp, chan]).astype(jnp.int32)
    images, size = features.shape[0], features.shape[1]
    group = images // c
    pixels = size * size
    count = float(images * pixels * d)
    rows = pixels * group
    deep = features.shape[3]
    mid, wide = conv_in.shape[1] * c, deep * c
    aligned = conv_out.shape[1] % LANES == 0

    fan_in, fan_out = conv_mid.shape[2:]
    classes = classifier.shape[1]
    space = -(-classes // LANES) * LANES
    tall = classifier.shape[0]
    laid = features.transpose(1, 2, 0, 3).reshape(pixels, images, deep)
    narrow_mid = conv_mid.reshape(9, fan_in, fan_out)
    sources = (laid, conv_in, narrow_mid, conv_out, classifier)
    own, mate, other, away, low_in, low_mid, low_head = call(
        functools.partial(prepare_kernel, c),
        [((rows, deep), BF16)] * c
        + [(conv_in.shape, BF16), ((13 if aligned else 9, fan_in, fan_out), BF16)]
        + [((tall * (space // LANES), LANES), BF16)],
        me, *sources, remain=5,
        scratch=[(x.shape, jnp.dtype(x.dtype).type) for x in sources],
        semaphores=[pltpu.SemaphoreType.DMA((5,))],
    )
    if not aligned:
        low_mid = jnp.concatenate([low_mid, conv_out.astype(BF16).reshape(4, fan_in, fan_out)])
    away, other = swap(away, 2, n), swap(other, 2, n)
    high_in = gather_high(low_in, n)
    pieces = [own, swap(mate, 1, n), other, swap(away, 1, n)]
    low_in, side_in = gather_low(high_in, False, n, (away, other))
    high_mid = gather_high(following(low_mid, high_in[1]), n)
    low_mid, side_mid = gather_low(high_mid, True, n, side_in)
    high_head = gather_high(following(low_head, side_mid), n)

    narrow = conv_in.shape[1]
    own = lax.dynamic_index_in_dim(labels.reshape(c, group), chan, 0, keepdims=False)
    own = jnp.concatenate([own, own])
    catalog = lax.broadcasted_iota(jnp.int32, (2 * group, class_weights.shape[0]), 1)
    chosen = catalog == own[:, None]
    weight_row = jnp.sum(jnp.where(chosen, class_weights[None, :], 0), axis=1).astype(F32)
    target = jnp.pad(
        chosen.astype(F32).reshape(2 * group, c, classes), ((0, 0), (0, 0), (0, space - classes))
    ).reshape(2 * group, c * space)
    own_weight = jnp.broadcast_to(0.5 * jnp.sum(weight_row), (1, mid))
    table = jnp.where(dp == 0, norms[:, 0], 0.0)
    table = jnp.where((jnp.arange(c) == chan)[None, :, None], table[:, None, :], 0.0)
    carried = table.reshape(-1, mid)
    own_weight = jnp.concatenate([own_weight, carried])

    def assembled(kernel, parts, *shapes):
        kernel = functools.partial(kernel, c, [masks for _, masks in parts])
        return call(kernel, [(shape, BF16) for shape in shapes], me, *[array for array, _ in parts])

    (whole_in,) = assembled(assemble_kernel, low_in, (wide, mid))
    feature_space = [((c, rows, deep), jnp.bfloat16)]
    feature_ends = [pltpu.SemaphoreType.DMA((c,))]
    hidden_one, sums_one = call(
        functools.partial(first_kernel, c),
        [((rows, mid), F32), ((2 + own_weight.shape[0], mid), F32)], me, own_weight, whole_in, *pieces,
        flops=2 * rows * wide * mid, scratch=feature_space, semaphores=feature_ends, remain=c,
    )
    sums_one, *_ = total(sums_one, n)
    weight_sum = sums_one[2, 0]
    tables = sums_one[3:].reshape(2, c, -1)
    norms_one = tables[:, :, :narrow].reshape(2, mid)
    norms_two = tables[:, :, narrow : 2 * narrow].reshape(2, mid)
    norms_three = tables[:, :, 2 * narrow :].reshape(2, wide)

    if aligned:
        whole_mid, whole_out = assembled(assemble_mid_kernel, low_mid, (9, mid, mid), (mid, wide))
    else:
        (whole_mid,) = assembled(assemble_mid_kernel, low_mid, (9, mid, mid))
        blocks = jnp.concatenate([array[:, 9:] for array, _ in low_mid])
        order = jnp.array([mask for _, masks in low_mid for mask in masks])
        blocks = jnp.take(blocks, jnp.argsort(order ^ number), axis=0)
        blocks = blocks.reshape((d, c) + conv_out.shape)
        whole_out = blocks.transpose(1, 2, 0, 3).reshape(mid, wide)
    whole_mid = whole_mid.reshape(9 * mid, mid)
    line = size * group
    padded = ((3, rows + 2 * line, mid), jnp.float32)
    many = ((rows, 9 * mid), jnp.bfloat16)
    act_one, hidden_two, sums_two = call(
        functools.partial(second_kernel, count, size, group),
        [((rows, mid), BF16), ((rows, mid), F32), ((2, mid), F32)],
        me, hidden_one, sums_one, norms_one, whole_mid,
        flops=18 * rows * mid * mid, scratch=[padded, many],
    )
    stack_head = following(jnp.stack(high_head), [low_mid[3][0], low_mid[4][0]])
    near_head, side_head = swap(stack_head, 2, n), swap(stack_head, 4, n)
    sums_two, middle_two = total(sums_two, n)
    hidden_two = following(hidden_two, near_head)

    act_two, hidden_three, sums_three = call(
        functools.partial(third_kernel, count),
        [((rows, mid), BF16), ((rows, wide), F32), ((2, wide), F32)],
        me, hidden_two, sums_two, norms_two, whole_out,
        flops=2 * rows * mid * wide,
    )
    sums_three, middle_three = total(sums_three, n)
    low_head = gather_cross(stack_head, near_head, side_head, n, middle_two)

    row_weights = jnp.stack([weight_row, weight_row / weight_sum], axis=1)
    upper_three, back_three, packed, _ = call(
        functools.partial(head_kernel, count, pixels, group, classes, c, [masks for _, masks in low_head]),
        [((rows, wide), F32), ((2, wide + LANES), F32), ((2 * group, (wide + c * space) // 2), BF16), ((1, 1), F32)],
        me, hidden_three, sums_three, norms_three, row_weights, target, *[array for array, _ in low_head], *pieces,
        flops=4 * 8 * wide * c * space, remain=len(low_head) + c,
        scratch=feature_space + [((wide, c * space), jnp.bfloat16), ((2 * group, wide), jnp.bfloat16)],
        semaphores=[pltpu.SemaphoreType.DMA((c + n * (space // LANES),))],
    )
    back_three, *_ = total(back_three, n)
    loss_sum = back_three[0, wide]

    down_three, upper_two, back_two = call(
        functools.partial(back_three_kernel, count),
        [((rows, wide), BF16), ((rows, mid), F32), ((2, mid), F32)],
        me, upper_three, hidden_three, sums_three, norms_three, back_three, whole_out,
        hidden_two, sums_two, norms_two,
        flops=2 * rows * mid * wide,
    )
    def blocks_of(shape):
        return [((n // 2,) + shape, BF16)] * 2

    masks = slot_masks(n)
    back_two, *_ = total(back_two, n)

    down_two, upper_one, back_one = call(
        functools.partial(back_two_kernel, count, size, group),
        [((rows, mid), BF16), ((rows, mid), F32), ((2, mid), F32)],
        me, upper_two, hidden_two, sums_two, norms_two, back_two, whole_mid,
        hidden_one, sums_one, norms_one,
        flops=18 * rows * mid * mid, scratch=[padded, many],
    )

    back_one = back_one + swap(back_one, 1, n)
    down_two = following(down_two, back_one)
    if aligned:
        parts_mid = call(
            functools.partial(grad_mid_kernel, c, masks, size, group), blocks_of((13, fan_in, fan_out)),
            me, act_one, down_two, act_two, down_three, flops=18 * rows * mid * mid,
            scratch=[((9, mid, mid), jnp.bfloat16), padded, many, ((mid, wide), jnp.bfloat16)],
        )
    else:
        pad = jnp.pad(act_one.reshape(size, size, group, mid), ((1, 1), (1, 1), (0, 0), (0, 0)))
        whole = [
            dot(pad[i : i + size, j : j + size].reshape(rows, mid), down_two, ((0,), (0,))).astype(BF16)
            for i in range(3)
            for j in range(3)
        ]
        whole = jnp.stack(whole).reshape(9, d, fan_in, c, fan_out).transpose(1, 3, 0, 2, 4)
        whole_two = dot(act_two, down_three, ((0,), (0,))).astype(BF16)
        whole_two = whole_two.reshape((c, conv_out.shape[0], d, conv_out.shape[1])).transpose(2, 0, 1, 3)
        whole_two = whole_two.reshape(d, c, 4, fan_in, fan_out)
        whole = jnp.concatenate([whole, whole_two], axis=2).reshape(n, 13, fan_in, fan_out)
        parts_mid = [jnp.take(whole, jnp.array(row) ^ number, axis=0) for row in masks]
    plan = [(0, 7, (4, 2)), (7, 13, (2, 4))]
    sends, keeps = split_start(*parts_mid, plan, n)
    back_one, half_way = total(back_one, n, sends[0], True)
    sends = following(sends, half_way)
    arrived = [swap(send, order[0], n) for send, (_, _, order) in zip(sends, plan)]
    sends, keeps = split_second(arrived, keeps, n)
    upper_one = following(upper_one, sends)
    parts_in = call(
        functools.partial(grad_in_kernel, count, c, masks), blocks_of(conv_in.shape),
        me, upper_one, hidden_one, sums_one, norms_one, back_one, *pieces,
        flops=2 * rows * mid * wide, remain=c, semaphores=feature_ends,
        scratch=[((wide, mid), jnp.bfloat16), ((rows, mid), jnp.bfloat16)] + feature_space,
    )
    arrived = [swap(send, order[1], n) for send, (_, _, order) in zip(sends, plan)]
    kept_in, *sends_in = scatter_start(*parts_in, n)
    sums_mid = split_third(arrived, keeps, plan, n)
    last_mid = scatter_last(sums_mid, n)
    arrived_in = [swap(send, mask, n) for send, mask in zip(sends_in, (2, 4, 6))]
    arrived_in, last_mid = lax.optimization_barrier((arrived_in, last_mid))
    sums_in = scatter_next(kept_in, arrived_in, n)
    last_mid = following(last_mid, sums_in[0])
    grad_mid = added(last_mid)
    grad_mid, grad_out = grad_mid[:9].reshape(conv_mid.shape), grad_mid[9:]
    if aligned:
        grad_out = grad_out.reshape(2, 2, fan_in, fan_out).transpose(0, 2, 1, 3)
    grad_out = grad_out.reshape(conv_out.shape)
    grad_in = added(scatter_last(sums_in, n))

    pairs, _ = gather_low(gather_high(packed, n), False, n)
    pairs = [(array, masks) for array, (_, masks) in zip(following([array for array, _ in pairs], sums_in[0]), pairs)]
    if aligned:
        (grad_head,) = call(
            functools.partial(grad_head_kernel, c, tall, space, group), [((tall, space), F32)],
            me, *[array for array, _ in pairs],
        )
    else:
        everything = jnp.concatenate([array for array, _ in pairs])
        everything = jnp.concatenate([everything[:, :group], everything[:, group:]], axis=2)
        everything = everything.reshape(-1, wide + c * space)
        pooled = lax.dynamic_slice_in_dim(everything, dp * tall, tall, axis=1)
        upper_logits = lax.dynamic_slice_in_dim(everything, wide + chan * space, space, axis=1)
        grad_head = dot(pooled, upper_logits, ((0,), (0,)))
    grad_head = grad_head[:, :classes]

    def mine(sums, width):
        return lax.dynamic_slice_in_dim(sums[:2], chan * width, width, axis=1)[::-1]

    grad_norms = jnp.concatenate(
        [mine(back_one, narrow), mine(back_two, narrow), mine(back_three, deep)], axis=1
    )[:, None, :]
    params = (conv_in, conv_mid, conv_out, classifier, norms)
    grads = (grad_in, grad_mid, grad_out, grad_head, grad_norms)
    moments = (momentum_in, momentum_mid, momentum_out, momentum_head, momentum_norms)
    averages = (average_in, average_mid, average_out, average_head, average_norms)
    rates = (RATE_MATRIX, RATE_MATRIX, RATE_MATRIX, RATE_MATRIX, RATE_NORM)
    results = [
        advance(p, g, m, a, r) for p, g, m, a, r in zip(params, grads, moments, averages, rates)
    ]
    news = [item[0] for item in results]
    freshs = [item[1] for item in results]
    means = [item[2] for item in results]
    copies = [item.astype(BF16) for item in news]
    return (loss_sum, weight_sum, *news, *freshs, *means, *copies)


def solution(mesh):
    matrices = (P("dp", "chan"), P(None, None, "dp", "chan"), P("chan", "dp"), P("dp", "chan"), P(None, "chan", None))
    return jax.shard_map(
        functools.partial(shards, mesh.shape["dp"], mesh.shape["chan"]),
        mesh=mesh,
        in_specs=(P("dp", None, None, "chan"), P("dp"), P()) + matrices * 3,
        out_specs=(P(), P()) + matrices * 4,
        check_vma=False,
    )
```
